512 devices in a mesh: pb: 32 (over z, core), ka: 16 (over y, x).
Axes of the slice: x: 4, y: 4, z: 16, core: 2. Of those that a mesh axis runs over, the one named last changes fastest.
Arguments:
- teacher_query: bfloat16 [16384, 256], P('pb'), may hold values from -96 to 96
- teacher_key: bfloat16 [16384, 256], P('ka'), may hold values from -8 to 8
- student_c: bfloat16 [16384, 128], P('pb'), may hold values from -0.009 to 0.009
- student_b: bfloat16 [16384, 128], P('ka'), may hold values from -0.009 to 0.009
- decay_rate: float32 [2, 16384], P(None, 'pb'), may hold values from 0 to 1
Outputs:
- grad_c: float32 [16384, 128], P(('pb', 'ka'))
- grad_b: float32 [16384, 128], P(('ka', 'pb'))
- grad_rate: float32 [2, 16384], P(None, 'pb')
The draws below stay inside these ranges and needn't reach their ends.
All inputs are finite; a program needn't handle non-finite values.
Results may differ from the reference program's by a relative error of at most 0.003.
Values may be sent and summed in bfloat16 or wider, within the bound.
A program may use at most 128 MiB of HBM per device.

```python
import math
import jax
import jax.numpy as jnp
from jax import lax

DH = 128
N = 64
H = 2
L = 16384


def row_scales(key):
    return jnp.exp(jax.random.uniform(key, (L, 1), jnp.float32, math.log(0.5), math.log(2.0)))


def run_factor(key):
    window = min(512, L // 4)
    stretch = window // 16
    windows = (L + window - 1) // window
    starts = jax.random.randint(key, (windows,), 0, window - stretch + 1)
    position = jnp.arange(L, dtype=jnp.int32)
    offset = position % window
    opening = starts[position // window]
    active = (offset >= opening) & (offset < opening + stretch)
    return jnp.where(active, 1.0, 0.1).astype(jnp.float32)[:, None]


def student_values(key, width):
    first, second = jax.random.split(key)
    factor = run_factor(second)
    values = jnp.clip(jax.random.normal(first, (L, width), jnp.float32), -3.0, 3.0)
    return (0.003 * factor * values).astype(jnp.bfloat16)


def draw_teacher_query(key, part):
    key = jax.random.fold_in(key, 5)
    first, second = jax.random.split(key)
    values = jnp.clip(jax.random.normal(first, (L, H * DH), jnp.float32), -4.0, 4.0) * row_scales(second)
    return values.astype(jnp.bfloat16)


def draw_teacher_key(key, part):
    key = jax.random.fold_in(key, 7)
    first, second = jax.random.split(key)
    values = jnp.clip(jax.random.normal(first, (L, H * DH), jnp.float32), -4.0, 4.0) * row_scales(second)
    return values.astype(jnp.bfloat16)


def draw_student_c(key, part):
    key = jax.random.fold_in(key, 11)
    return student_values(key, H * N)


def draw_student_b(key, part):
    key = jax.random.fold_in(key, 13)
    return student_values(key, H * N)


def draw_decay_rate(key, part):
    key = jax.random.fold_in(key, 9)
    keys = jax.random.split(key, 5)
    local = jnp.exp(jax.random.uniform(keys[0], (H, L), jnp.float32, math.log(0.5), math.log(1.5)))
    regional = jnp.exp(jax.random.uniform(keys[1], (H, L // 128), jnp.float32, math.log(0.5), math.log(1.5)))
    regional = jnp.repeat(regional, 128, axis=1)
    slow = 0.3 / L
    order = jax.random.permutation(keys[2], H)
    base = jnp.where(order == 0, 0.03, slow).astype(jnp.float32)
    rate = base[:, None] * local * regional
    spots = jax.random.randint(keys[3], (H, 3), 0, L)
    amount = -jnp.log(1.0 - jax.random.uniform(keys[4], (H, 3), jnp.float32, 0.2, 0.4))
    rate = rate.at[jnp.arange(H)[:, None], spots].add(amount)
    return rate.astype(jnp.float32)


def setup_inputs(seed: int = 0) -> dict:
    splits = jax.random.split(jax.random.key(seed), 6)
    teacher_query = draw_teacher_query(jax.random.fold_in(splits[5], 71), 0)
    teacher_key = draw_teacher_key(jax.random.fold_in(splits[5], 71), 0)
    student_c = draw_student_c(jax.random.fold_in(splits[5], 71), 0)
    student_b = draw_student_b(jax.random.fold_in(splits[5], 71), 0)
    decay_rate = draw_decay_rate(jax.random.fold_in(splits[5], 71), 0)
    return dict(teacher_query=teacher_query, teacher_key=teacher_key, student_c=student_c, student_b=student_b, decay_rate=decay_rate)


def reference(teacher_query, teacher_key, student_c, student_b, decay_rate):
    total = teacher_query.shape[0]
    heads = decay_rate.shape[0]
    cum = -jnp.cumsum(decay_rate, axis=1)
    query_all = teacher_query.astype(jnp.float32).reshape(total, heads, -1)
    key_all = teacher_key.astype(jnp.float32).reshape(total, heads, -1)
    c_all = student_c.astype(jnp.float32).reshape(total, heads, -1)
    b_all = student_b.astype(jnp.float32).reshape(total, heads, -1)
    state = c_all.shape[2]
    scale = 1.0 / math.sqrt(query_all.shape[2])
    block = min(total, 512)
    count = total // block
    key_pos = jnp.arange(total, dtype=jnp.int32)
    factor = 2.0 * total

    def step(carry, index):
        grad_b, col_sums = carry
        start = (index * block).astype(jnp.int32)
        query_rows = lax.dynamic_slice_in_dim(query_all, start, block, 0)
        c_rows = lax.dynamic_slice_in_dim(c_all, start, block, 0)
        cum_rows = lax.dynamic_slice_in_dim(cum, start, block, 1)
        query_pos = start + jnp.arange(block, dtype=jnp.int32)
        mask = (query_pos[:, None] >= key_pos[None, :])[None]
        scores = jnp.einsum('qhd,khd->hqk', query_rows, key_all) * scale
        masked = jnp.where(mask, scores, -1e+30)
        peak = lax.optimization_barrier(jnp.max(masked, axis=2, keepdims=True))
        expo = jnp.where(mask, jnp.exp(masked - peak), 0.0)
        prob = expo / lax.optimization_barrier(jnp.sum(expo, axis=2, keepdims=True))
        decay = jnp.exp(jnp.where(mask, cum_rows[:, :, None] - cum[:, None, :], -1e+30))
        inner = jnp.einsum('qhn,khn->hqk', c_rows, b_all)
        student = inner * decay
        grad = factor * (student - prob)
        weight = lax.optimization_barrier((grad * decay).astype(jnp.bfloat16)).astype(jnp.float32)
        grad_c = jnp.einsum('hqk,khn->qhn', weight, b_all)
        grad_b = grad_b + jnp.einsum('hqk,qhn->khn', weight, c_rows)
        related = grad * student
        row_sums = lax.optimization_barrier(jnp.sum(related, axis=2))
        col_sums = col_sums + lax.optimization_barrier(jnp.sum(related, axis=1))
        return ((grad_b, col_sums), (grad_c, row_sums))
    start_carry = (jnp.zeros((total, heads, state), jnp.float32), jnp.zeros((heads, total), jnp.float32))
    (grad_b, col_sums), (grad_c, row_sums) = lax.scan(step, start_carry, jnp.arange(count, dtype=jnp.int32))
    grad_c = grad_c.reshape(total, heads * state)
    grad_b = grad_b.reshape(total, heads * state)
    row_sums = jnp.moveaxis(row_sums, 0, 1).reshape(heads, total)
    slope = row_sums - col_sums
    tail = jnp.cumsum(slope[:, ::-1], axis=1)[:, ::-1]
    return (grad_c, grad_b, -tail)
```

```python
import functools
import math

import jax
import jax.numpy as jnp
from jax import lax
from jax.experimental import pallas as pl
from jax.experimental.pallas import tpu as pltpu
from jax.sharding import PartitionSpec as P

MESH = pl.DeviceIdType.MESH
NEGATIVE = -1e30
LOG2E = 1.0 / math.log(2.0)
CHUNK = 128


def dot(a, b, dims):
    return lax.dot_general(a, b, (dims, ((), ())), preferred_element_type=jnp.float32)


def fold_rows(x):
    return jnp.sum(x.reshape(x.shape[0] // 8, 8, x.shape[1]), axis=0)


def fold_lanes(x):
    width = x.shape[1]
    out = x[:, 0:128]
    for k in range(128, width, 128):
        out = out + x[:, k : k + 128]
    return out


def lane_prefix(x):
    width = x.shape[1]
    lane = lax.broadcasted_iota(jnp.int32, x.shape, 1)
    shift = 1
    while shift < width:
        x = x + jnp.where(lane >= shift, pltpu.roll(x, shift, 1), 0.0)
        shift *= 2
    return x


def kernel(
    nb,
    na,
    heads,
    q_hbm,
    k_hbm,
    c_hbm,
    b_hbm,
    rate_ref,
    gc_ref,
    gb_ref,
    gr_ref,
    q_ref,
    k_ref,
    c_ref,
    b_ref,
    ch_ref,
    bt_ref,
    s_ref,
    w_ref,
    kcol_ref,
    rel_ref,
    scan_ref,
    rates_ref,
    stat_ref,
    fold_ref,
    colsend_ref,
    col_ref,
    slope_ref,
    gbown_ref,
    gbsend_ref,
    gbrecv_ref,
    gcown_ref,
    gcsend_ref,
    gcrecv_ref,
    in_sem,
    rate_send,
    rate_recv,
    stat_send,
    stat_recv,
    fold_send,
    fold_recv,
    col_send,
    col_recv,
    slope_send,
    slope_recv,
    gb_send,
    gb_recv,
    gc_send,
    gc_recv,
):
    pb = lax.axis_index("pb")
    ka = lax.axis_index("ka")
    qn, width = q_ref.shape
    kn = k_ref.shape[0]
    dh = width // heads
    state = c_ref.shape[1] // heads
    ratio = kn // qn
    steps = kn // CHUNK
    gb_rows = kn // nb
    gc_rows = qn // na
    per_chunk = CHUNK // gb_rows
    factor = 2.0 * qn * nb
    first = ratio * ka
    live = pb >= first
    plane_live = pb // ratio

    loads = [
        pltpu.make_async_copy(src, dst, in_sem.at[n])
        for n, (src, dst) in enumerate(
            ((q_hbm, q_ref), (k_hbm, k_ref), (c_hbm, c_ref), (b_hbm, b_ref))
        )
    ]
    for load in loads:
        load.start()

    rates_ref[...] = jnp.zeros_like(rates_ref)
    rates_ref[pb] = rate_ref[...]
    fold_ref[...] = jnp.zeros_like(fold_ref)
    slope_ref[...] = jnp.zeros_like(slope_ref)
    col_ref[...] = jnp.zeros_like(col_ref)
    stat_ref[...] = jnp.concatenate(
        [
            jnp.full((na, heads, qn), NEGATIVE, jnp.float32),
            jnp.zeros((na, heads, qn), jnp.float32),
        ],
        axis=1,
    )

    barrier = pltpu.get_barrier_semaphore()

    @pl.loop(1, na)
    def _(k):
        pl.semaphore_signal(
            barrier, inc=1, device_id=(pb, lax.rem(ka + k, na)), device_id_type=MESH
        )

    @pl.loop(1, nb)
    def _(k):
        pl.semaphore_signal(
            barrier, inc=1, device_id=(lax.rem(pb + k, nb), ka), device_id_type=MESH
        )

    def rate_copy(slot, target):
        return pltpu.make_async_remote_copy(
            src_ref=rates_ref.at[slot],
            dst_ref=rates_ref.at[slot],
            send_sem=rate_send.at[target],
            recv_sem=rate_recv.at[slot],
            device_id=(target, ka),
            device_id_type=MESH,
        )

    def stat_copy(slot, target):
        return pltpu.make_async_remote_copy(
            src_ref=stat_ref.at[slot],
            dst_ref=stat_ref.at[slot],
            send_sem=stat_send.at[target],
            recv_sem=stat_recv.at[slot],
            device_id=(pb, target),
            device_id_type=MESH,
        )

    def fold_copy(slot, target):
        return pltpu.make_async_remote_copy(
            src_ref=fold_ref.at[slot],
            dst_ref=fold_ref.at[slot],
            send_sem=fold_send.at[target],
            recv_sem=fold_recv.at[slot],
            device_id=(target, ka),
            device_id_type=MESH,
        )

    def col_copy(part, slot):
        return pltpu.make_async_remote_copy(
            src_ref=colsend_ref.at[part],
            dst_ref=col_ref.at[slot],
            send_sem=col_send.at[part],
            recv_sem=col_recv.at[slot],
            device_id=(first + part, ka),
            device_id_type=MESH,
        )

    def slope_copy(slot, target):
        return pltpu.make_async_remote_copy(
            src_ref=slope_ref.at[slot],
            dst_ref=slope_ref.at[slot],
            send_sem=slope_send.at[target],
            recv_sem=slope_recv.at[slot],
            device_id=(pb, target),
            device_id_type=MESH,
        )

    def gb_copy(slot, target):
        return pltpu.make_async_remote_copy(
            src_ref=gbsend_ref.at[target],
            dst_ref=gbrecv_ref.at[slot],
            send_sem=gb_send.at[target],
            recv_sem=gb_recv.at[slot],
            device_id=(target, ka),
            device_id_type=MESH,
        )

    def gc_copy(slot, target):
        return pltpu.make_async_remote_copy(
            src_ref=gcsend_ref.at[target],
            dst_ref=gcrecv_ref.at[slot],
            send_sem=gc_send.at[target],
            recv_sem=gc_recv.at[slot],
            device_id=(pb, target),
            device_id_type=MESH,
        )

    offset = pb * qn - ka * kn

    def mask_of(t):
        rows = lax.broadcasted_iota(jnp.int32, (CHUNK, qn), 0)
        cols = lax.broadcasted_iota(jnp.int32, (CHUNK, qn), 1)
        return cols - rows >= t * CHUNK - offset

    def chunk_rows(t):
        return pl.ds(pl.multiple_of(t * CHUNK, CHUNK), CHUNK)

    loads[0].wait()
    loads[1].wait()
    scale2 = LOG2E / math.sqrt(dh)

    @pl.when(live)
    def _():
        for h in range(heads):
            lanes = slice(h * dh, (h + 1) * dh)

            def score_turn(t, peak, h=h, lanes=lanes):
                s = dot(k_ref[chunk_rows(t), lanes], q_ref[:, lanes], ((1,), (1,)))
                s = jnp.where(mask_of(t), s * scale2, NEGATIVE)
                s_ref[h, chunk_rows(t), :] = s
                return jnp.maximum(peak, jnp.max(s.reshape(CHUNK // 8, 8, qn), axis=0))

            peak = lax.fori_loop(
                0, steps, score_turn, jnp.full((8, qn), NEGATIVE, jnp.float32)
            )
            peak = jnp.max(peak, axis=0, keepdims=True)

            def expo_turn(t, total, h=h, peak=peak):
                e = jnp.exp2(s_ref[h, chunk_rows(t), :] - peak)
                s_ref[h, chunk_rows(t), :] = e
                return total + fold_rows(e)

            total = lax.fori_loop(0, steps, expo_turn, jnp.zeros((8, qn), jnp.float32))
            stat_ref[ka, h : h + 1, :] = peak
            stat_ref[ka, heads + h : heads + h + 1, :] = jnp.sum(
                total, axis=0, keepdims=True
            )

    loads[2].wait()
    loads[3].wait()
    pl.semaphore_wait(barrier, na + nb - 2)

    @pl.when(live)
    def _():
        @pl.loop(1, na)
        def _(k):
            target = lax.rem(ka + k, na)

            @pl.when(target <= plane_live)
            def _():
                stat_copy(ka, target).start()

        @pl.loop(pb + 1, nb)
        def _(target):
            rate_copy(pb, target).start()

        head_of = lax.broadcasted_iota(jnp.int32, (qn, heads * state), 1) // state
        c_all = c_ref[...]
        for h in range(heads):
            ch_ref[h] = jnp.where(head_of == h, c_all, jnp.zeros_like(c_all))
        bt_ref[...] = jnp.transpose(b_ref[...])

        @pl.loop(first, pb)
        def _(slot):
            rate_copy(slot, slot).wait_recv()

        scan_ref[...] = jnp.zeros_like(scan_ref)
        scan_ref[0:heads, :] = rate_ref[...]
        for part in range(ratio):
            low = heads * (1 + part)
            scan_ref[low : low + heads, :] = rates_ref[first + part]
        rates = scan_ref[...]
        scan_ref[...] = lane_prefix(rates)
        ends = jnp.sum(rates, axis=1, keepdims=True)
        before = jnp.sum(
            jnp.sum(rates_ref[...], axis=0) - rate_ref[...], axis=1, keepdims=True
        )
        for part in range(ratio):
            pass
        for h in range(heads):
            shift = jnp.zeros((1, 1), jnp.float32)
            for part in range(ratio):
                row = heads * (1 + part) + h
                prefix = (scan_ref[row : row + 1, :] + shift) * LOG2E
                kcol_ref[h, part * qn : (part + 1) * qn, :] = jnp.transpose(
                    jnp.broadcast_to(prefix, (128, qn))
                )
                shift = shift + ends[row : row + 1, :]
        arow = (scan_ref[0:heads, :] + before) * LOG2E

        @pl.loop(0, plane_live + 1)
        def _(slot):
            @pl.when(slot != ka)
            def _():
                stat_copy(slot, slot).wait_recv()

        peaks = stat_ref[:, 0:heads, :]
        totals = stat_ref[:, heads : 2 * heads, :]
        peak = jnp.max(peaks, axis=0)
        total = jnp.sum(totals * jnp.exp2(peaks - peak[None]), axis=0)
        own_peak = stat_ref[ka, 0:heads, :]
        scaling = jnp.exp2(own_peak - peak) / total

        def grad_turn(n, row_sums):
            t = lax.rem(n + pb * gb_rows // CHUNK, steps)
            rows = chunk_rows(t)
            mask = mask_of(t)
            b_rows = b_ref[rows, :]
            out = jnp.zeros((CHUNK, heads * state), jnp.float32)
            new_sums = []
            for h in range(heads):
                inner = dot(b_rows, ch_ref[h], ((1,), (1,)))
                gap = jnp.concatenate(
                    [kcol_ref[h, rows, :]] * (qn // 128), axis=1
                ) - arow[h : h + 1, :]
                decay = jnp.exp2(jnp.where(mask, gap, NEGATIVE))
                student = inner * decay
                grad = student - s_ref[h, rows, :] * scaling[h : h + 1, :]
                weight = (grad * decay).astype(jnp.bfloat16)
                w_ref[h, rows, :] = weight
                related = grad * student
                rel_ref[h, rows, :] = fold_lanes(related)
                new_sums.append(row_sums[h] + fold_rows(related))
                out = out + dot(weight, ch_ref[h], ((1,), (0,)))
            out = out * factor
            for part in range(per_chunk):
                target = t * per_chunk + part
                piece = out[part * gb_rows : (part + 1) * gb_rows, :]
                gbsend_ref[target] = piece.astype(jnp.bfloat16)

                @pl.when(target == pb)
                def _(piece=piece):
                    gbown_ref[...] = piece

                @pl.when(target != pb)
                def _(target=target):
                    gb_copy(pb, target).start()

            return tuple(new_sums)

        row_sums = lax.fori_loop(
            0,
            steps,
            grad_turn,
            tuple(jnp.zeros((8, qn), jnp.float32) for _ in range(heads)),
        )

        fold = jnp.zeros((heads, 128), jnp.float32)
        for part in range(ratio):
            for h in range(heads):
                flipped = jnp.transpose(rel_ref[h, part * qn : (part + 1) * qn, :])
                sums = jnp.sum(flipped, axis=0, keepdims=True)
                colsend_ref[part, h : h + 1, :] = sums
            fold = fold + fold_lanes(colsend_ref[part])
        fold_ref[pb] = fold

        @pl.loop(first, pb)
        def _(target):
            fold_copy(pb, target).start()

        for part in range(ratio):

            @pl.when(pb != first + part)
            def _(part=part):
                col_copy(part, pb).start()

            @pl.when(pb == first + part)
            def _(part=part):
                col_ref[pb] = colsend_ref[part]

        for h in range(heads):
            slope_ref[ka, h : h + 1, 0:qn] = jnp.sum(
                row_sums[h], axis=0, keepdims=True
            )
            flat = dot(
                bt_ref[h * state : (h + 1) * state, :], w_ref[h], ((1,), (0,))
            )
            scan_t = jnp.transpose(flat * factor)
            gcown_ref[:, h * state : (h + 1) * state] = scan_t

        for target in range(na):
            gcsend_ref[target] = gcown_ref[
                target * gc_rows : (target + 1) * gc_rows, :
            ].astype(jnp.bfloat16)

        @pl.loop(1, na)
        def _(k):
            gc_copy(ka, lax.rem(ka + k, na)).start()

        @pl.loop(pb + 1, nb)
        def _(slot):
            fold_copy(slot, slot).wait_recv()

        slot_of = lax.broadcasted_iota(jnp.int32, (nb, 1, 1), 0)
        later = jnp.where(slot_of > pb, fold_ref[...], 0.0)
        slope_ref[ka, :, qn:] = jnp.sum(later, axis=0)

        @pl.when(plane_live == ka)
        def _():
            part = pb - first

            @pl.loop(first, nb)
            def _(slot):
                @pl.when(slot != pb)
                def _():
                    pltpu.make_async_remote_copy(
                        src_ref=colsend_ref.at[0],
                        dst_ref=col_ref.at[slot],
                        send_sem=col_send.at[0],
                        recv_sem=col_recv.at[slot],
                        device_id=(slot, ka),
                        device_id_type=MESH,
                    ).wait_recv()

            everything = jnp.sum(col_ref[...], axis=0)
            slope_ref[ka, :, 0:qn] = slope_ref[ka, :, 0:qn] - everything
            inside = fold_lanes(everything - col_ref[pb])

            @pl.when(part < ratio - 1)
            def _():
                slope_ref[ka, :, qn:] = inside

        @pl.loop(1, na)
        def _(k):
            slope_copy(ka, lax.rem(ka + k, na)).start()

    gc_ref[...] = jnp.zeros_like(gc_ref)

    @pl.when(live)
    def _():
        gc_ref[...] = gcown_ref[
            pl.ds(pl.multiple_of(ka * gc_rows, gc_rows), gc_rows), :
        ]

    @pl.loop(0, plane_live + 1)
    def _(slot):
        @pl.when(slot != ka)
        def _():
            gc_copy(slot, slot).wait_recv()
            gc_ref[...] += gcrecv_ref[slot].astype(jnp.float32)

    gb_ref[...] = jnp.zeros_like(gb_ref)

    @pl.when(live)
    def _():
        gb_ref[...] = gbown_ref[...]

    @pl.loop(first, nb)
    def _(slot):
        @pl.when(slot != pb)
        def _():
            gb_copy(slot, slot).wait_recv()
            gb_ref[...] += gbrecv_ref[slot].astype(jnp.float32)

    @pl.loop(0, plane_live + 1)
    def _(slot):
        @pl.when(slot != ka)
        def _():
            slope_copy(slot, slot).wait_recv()

    both = jnp.sum(slope_ref[...], axis=0)
    slope = both[:, 0:qn]
    after = jnp.sum(both[:, qn:], axis=1, keepdims=True)
    scan_ref[...] = jnp.zeros_like(scan_ref)
    scan_ref[0:heads, :] = slope
    suffix = jnp.sum(slope, axis=1, keepdims=True) - lane_prefix(scan_ref[...])[0:heads, :]
    gr_ref[...] = -factor * (suffix + slope + after)

    @pl.when(live)
    def _():
        @pl.loop(pb + 1, nb)
        def _(target):
            rate_copy(pb, target).wait_send()

        @pl.loop(first, pb)
        def _(target):
            fold_copy(pb, target).wait_send()

        for part in range(ratio):

            @pl.when(pb != first + part)
            def _(part=part):
                col_copy(part, pb).wait_send()

        @pl.loop(0, na)
        def _(target):
            @pl.when(target != ka)
            def _():
                @pl.when(target <= plane_live)
                def _():
                    stat_copy(ka, target).wait_send()

                gc_copy(ka, target).wait_send()
                slope_copy(ka, target).wait_send()

        @pl.loop(0, nb)
        def _(target):
            @pl.when(target != pb)
            def _():
                gb_copy(pb, target).wait_send()


def body(teacher_query, teacher_key, student_c, student_b, decay_rate):
    heads = decay_rate.shape[0]
    nb = lax.axis_size("pb")
    na = lax.axis_size("ka")
    qn, width = teacher_query.shape
    kn = teacher_key.shape[0]
    cols = student_c.shape[1]
    ratio = kn // qn
    f32, bf16 = jnp.float32, jnp.bfloat16
    vmem = pl.BlockSpec(memory_space=pltpu.VMEM)
    hbm = pl.BlockSpec(memory_space=pl.ANY)
    dma = pltpu.SemaphoreType.DMA
    scan_rows = -(-heads * (1 + ratio) // 8) * 8
    return pl.pallas_call(
        functools.partial(kernel, nb, na, heads),
        out_shape=(
            jax.ShapeDtypeStruct((qn // na, cols), f32),
            jax.ShapeDtypeStruct((kn // nb, cols), f32),
            jax.ShapeDtypeStruct((heads, qn), f32),
        ),
        in_specs=[hbm, hbm, hbm, hbm, vmem],
        out_specs=[vmem, vmem, vmem],
        scratch_shapes=[
            pltpu.VMEM((qn, width), bf16),
            pltpu.VMEM((kn, width), bf16),
            pltpu.VMEM((qn, cols), bf16),
            pltpu.VMEM((kn, cols), bf16),
            pltpu.VMEM((heads, qn, cols), bf16),
            pltpu.VMEM((cols, kn), bf16),
            pltpu.VMEM((heads, kn, qn), f32),
            pltpu.VMEM((heads, kn, qn), bf16),
            pltpu.VMEM((heads, kn, 128), f32),
            pltpu.VMEM((heads, kn, 128), f32),
            pltpu.VMEM((scan_rows, qn), f32),
            pltpu.VMEM((nb, heads, qn), f32),
            pltpu.VMEM((na, 2 * heads, qn), f32),
            pltpu.VMEM((nb, heads, 128), f32),
            pltpu.VMEM((ratio, heads, qn), f32),
            pltpu.VMEM((nb, heads, qn), f32),
            pltpu.VMEM((na, heads, qn + 128), f32),
            pltpu.VMEM((kn // nb, cols), f32),
            pltpu.VMEM((nb, kn // nb, cols), bf16),
            pltpu.VMEM((nb, kn // nb, cols), bf16),
            pltpu.VMEM((qn, cols), f32),
            pltpu.VMEM((na, qn // na, cols), bf16),
            pltpu.VMEM((na, qn // na, cols), bf16),
            dma((4,)),
            dma((nb,)),
            dma((nb,)),
            dma((na,)),
            dma((na,)),
            dma((nb,)),
            dma((nb,)),
            dma((ratio,)),
            dma((nb,)),
            dma((na,)),
            dma((na,)),
            dma((nb,)),
            dma((nb,)),
            dma((na,)),
            dma((na,)),
        ],
        compiler_params=pltpu.CompilerParams(
            collective_id=0, has_side_effects=True, vmem_limit_bytes=48 * 1024 * 1024
        ),
    )(teacher_query, teacher_key, student_c, student_b, decay_rate)


def solution(mesh):
    placed = (P("pb", None), P("ka", None), P("pb", None), P("ka", None), P(None, "pb"))
    return jax.shard_map(
        body,
        mesh=mesh,
        in_specs=placed,
        out_specs=(P(("pb", "ka"), None), P(("ka", "pb"), None), P(None, "pb")),
        check_vma=False,
    )
```

```python
import functools
import math

import jax
import jax.numpy as jnp
from jax import lax
from jax.experimental import pallas as pl
from jax.experimental.pallas import tpu as pltpu
from jax.sharding import PartitionSpec as P

MESH = pl.DeviceIdType.MESH
NEGATIVE = -1e30
LOG2E = 1.0 / math.log(2.0)
CHUNK = 128


def dot(a, b, dims):
    return lax.dot_general(a, b, (dims, ((), ())), preferred_element_type=jnp.float32)


def fold_rows(x):
    return jnp.sum(x.reshape(x.shape[0] // 8, 8, x.shape[1]), axis=0)


def fold_lanes(x):
    width = x.shape[1]
    out = x[:, 0:128]
    for k in range(128, width, 128):
        out = out + x[:, k : k + 128]
    return out


def lane_prefix(x):
    width = x.shape[1]
    lane = lax.broadcasted_iota(jnp.int32, x.shape, 1)
    shift = 1
    while shift < width:
        x = x + jnp.where(lane >= shift, pltpu.roll(x, shift, 1), 0.0)
        shift *= 2
    return x


def kernel(
    nb,
    na,
    heads,
    q_hbm,
    k_hbm,
    c_hbm,
    b_hbm,
    rate_hbm,
    gc_ref,
    gb_ref,
    gr_ref,
    q_ref,
    k_ref,
    c_ref,
    b_ref,
    ch_ref,
    bt_ref,
    s_ref,
    w_ref,
    kcol_ref,
    scan_ref,
    pair_ref,
    krate_ref,
    rfold_ref,
    stat_ref,
    cs_ref,
    cssib_ref,
    fold_ref,
    colsend_ref,
    col_ref,
    slope_ref,
    gbpart_ref,
    gbsib_ref,
    gbown_ref,
    gbsend_ref,
    gbrecv_ref,
    gcown_ref,
    gcsend_ref,
    gcrecv_ref,
    in_sem,
    pair_send,
    pair_recv,
    rate_send,
    krate_recv,
    rfold_recv,
    stat_send,
    stat_recv,
    cs_send,
    cs_recv,
    fold_send,
    fold_recv,
    col_send,
    col_recv,
    slope_send,
    slope_recv,
    gx_send,
    gx_recv,
    gb_send,
    gb_recv,
    gc_send,
    gc_recv,
):
    pb = lax.axis_index("pb")
    ka = lax.axis_index("ka")
    qn, width = q_ref.shape
    kn = k_ref.shape[0]
    dh = width // heads
    cols = c_ref.shape[1]
    state = cols // heads
    nz = nb // 2
    z = pb // 2
    core = lax.rem(pb, 2)
    other = 1 - core
    sibling = 2 * z + other
    steps = kn // CHUNK
    half = steps // 2
    gb_rows = kn // nb
    gc_rows = qn // na
    per_chunk = CHUNK // (2 * gb_rows)
    factor = 2.0 * qn * nb
    live = z >= ka
    diagonal = z == ka

    loads = [
        pltpu.make_async_copy(src, dst, in_sem.at[n])
        for n, (src, dst) in enumerate(
            (
                (q_hbm, q_ref),
                (k_hbm, k_ref),
                (rate_hbm, pair_ref.at[core]),
                (c_hbm, c_ref),
                (b_hbm, b_ref),
            )
        )
    ]
    for load in loads:
        load.start()

    barrier = pltpu.get_barrier_semaphore()
    pl.semaphore_signal(barrier, inc=1, device_id=(sibling, ka), device_id_type=MESH)

    @pl.loop(1, na)
    def _(k):
        pl.semaphore_signal(
            barrier, inc=1, device_id=(pb, lax.rem(ka + k, na)), device_id_type=MESH
        )

    @pl.loop(1, nz)
    def _(k):
        pl.semaphore_signal(
            barrier,
            inc=1,
            device_id=(2 * lax.rem(z + k, nz) + core, ka),
            device_id_type=MESH,
        )

    def to(src, dst, send, recv, device):
        return pltpu.make_async_remote_copy(
            src_ref=src,
            dst_ref=dst,
            send_sem=send,
            recv_sem=recv,
            device_id=device,
            device_id_type=MESH,
        )

    def up(target):
        return (2 * target + core, ka)

    def pair_copy(slot):
        return to(
            pair_ref.at[slot], pair_ref.at[slot], pair_send, pair_recv, (sibling, ka)
        )

    def krate_copy(target):
        return to(pair_ref, krate_ref, rate_send.at[target], krate_recv, up(target))

    def rfold_copy(slot, target):
        return to(
            rfold_ref.at[slot],
            rfold_ref.at[slot],
            rate_send.at[target],
            rfold_recv.at[slot],
            up(target),
        )

    def stat_copy(slot, target):
        return to(
            stat_ref.at[slot],
            stat_ref.at[slot],
            stat_send.at[target],
            stat_recv.at[slot],
            (pb, target),
        )

    def cs_copy():
        return to(cs_ref, cssib_ref, cs_send, cs_recv, (sibling, ka))

    def fold_copy(slot, target):
        return to(
            fold_ref.at[slot],
            fold_ref.at[slot],
            fold_send.at[target],
            fold_recv.at[slot],
            up(target),
        )

    def col_copy(slot):
        return to(
            colsend_ref, col_ref.at[slot], col_send, col_recv.at[slot], up(ka)
        )

    def slope_copy(slot, target):
        return to(
            slope_ref.at[slot],
            slope_ref.at[slot],
            slope_send,
            slope_recv.at[slot],
            (pb, target),
        )

    def gx_copy(start, count):
        return to(
            gbpart_ref.at[pl.ds(start, count), other],
            gbsib_ref.at[pl.ds(start, count)],
            gx_send,
            gx_recv,
            (sibling, ka),
        )

    def gb_copy(slot, target):
        return to(
            gbsend_ref.at[target],
            gbrecv_ref.at[slot],
            gb_send,
            gb_recv.at[slot],
            up(target),
        )

    def gc_copy(slot, target):
        return to(
            gcsend_ref.at[target],
            gcrecv_ref.at[slot],
            gc_send,
            gc_recv.at[slot],
            (pb, target),
        )

    offset = pb * qn - ka * kn

    def mask_of(t):
        rows = lax.broadcasted_iota(jnp.int32, (CHUNK, qn), 0)
        lanes = lax.broadcasted_iota(jnp.int32, (CHUNK, qn), 1)
        return lanes - rows >= t * CHUNK - offset

    def chunk_rows(t):
        return pl.ds(pl.multiple_of(t * CHUNK, CHUNK), CHUNK)

    scale2 = LOG2E / math.sqrt(dh)

    def head_stats(h):
        lanes = slice(h * dh, (h + 1) * dh)

        def score_turn(t, peak):
            s = dot(k_ref[chunk_rows(t), lanes], q_ref[:, lanes], ((1,), (1,)))
            s = jnp.where(mask_of(t), s * scale2, NEGATIVE)
            s_ref[h, chunk_rows(t), :] = s
            return jnp.maximum(peak, jnp.max(s.reshape(CHUNK // 8, 8, qn), axis=0))

        peak = lax.fori_loop(
            0, steps, score_turn, jnp.full((8, qn), NEGATIVE, jnp.float32)
        )
        peak = jnp.max(peak, axis=0, keepdims=True)

        def expo_turn(t, total):
            e = jnp.exp2(s_ref[h, chunk_rows(t), :] - peak)
            s_ref[h, chunk_rows(t), :] = e
            return total + fold_rows(e)

        total = lax.fori_loop(0, steps, expo_turn, jnp.zeros((8, qn), jnp.float32))
        stat_ref[ka, h : h + 1, :] = peak
        stat_ref[ka, heads + h : heads + h + 1, :] = jnp.sum(
            total, axis=0, keepdims=True
        )

    @pl.when(live)
    def _():
        stat_init = jnp.concatenate(
            [
                jnp.full((heads, qn), NEGATIVE, jnp.float32),
                jnp.zeros((heads, qn), jnp.float32),
            ],
            axis=0,
        )

        @pl.loop(z + 1, na)
        def _(slot):
            stat_ref[slot] = stat_init

    loads[0].wait()
    loads[1].wait()

    @pl.when(live)
    def _():
        for h in range(heads // 2):
            head_stats(h)

    for load in loads[2:]:
        load.wait()
    pl.semaphore_wait(barrier, na + nz - 1)

    @pl.when(live)
    def _():
        pair_copy(core).start()
        for h in range(heads // 2, heads):
            head_stats(h)

        @pl.loop(1, na)
        def _(k):
            target = lax.rem(ka + k, na)

            @pl.when(target <= z)
            def _():
                stat_copy(ka, target).start()

        pair_copy(other).wait_recv()
        own_fold = jnp.stack([fold_lanes(pair_ref[0]), fold_lanes(pair_ref[1])])
        rfold_ref[z] = own_fold

        @pl.loop(z + 1, nz)
        def _(target):
            @pl.when(diagonal)
            def _():
                krate_copy(target).start()

            @pl.when(jnp.logical_not(diagonal))
            def _():
                rfold_copy(z, target).start()

        head_of = lax.broadcasted_iota(jnp.int32, (qn, cols), 1) // state
        c_all = c_ref[...]
        for h in range(heads):
            ch_ref[h] = jnp.where(head_of == h, c_all, jnp.zeros_like(c_all))
        bt_ref[...] = jnp.transpose(b_ref[...])

        scan_ref[...] = jnp.zeros_like(scan_ref)
        scan_ref[0:heads, :] = pair_ref[core]

        @pl.when(diagonal)
        def _():
            for part in range(2):
                low = heads * (1 + part)
                scan_ref[low : low + heads, :] = pair_ref[part]

        @pl.when(jnp.logical_not(diagonal))
        def _():
            krate_copy(z).wait_recv()
            for part in range(2):
                low = heads * (1 + part)
                scan_ref[low : low + heads, :] = krate_ref[part]

        rates = scan_ref[...]
        scan_ref[...] = lane_prefix(rates)
        ends = jnp.sum(rates, axis=1, keepdims=True)
        for h in range(heads):
            shift = jnp.zeros((1, 1), jnp.float32)
            for part in range(2):
                row = heads * (1 + part) + h
                prefix = (scan_ref[row : row + 1, :] + shift) * LOG2E
                kcol_ref[h, part * qn : (part + 1) * qn, :] = jnp.transpose(
                    jnp.broadcast_to(prefix, (128, qn))
                )
                shift = shift + ends[row : row + 1, :]

        def between_turn(slot, total):
            rfold_copy(slot, z).wait_recv()
            return total + rfold_ref[slot, 0] + rfold_ref[slot, 1]

        between = lax.fori_loop(
            ka + 1, z, between_turn, jnp.zeros((heads, 128), jnp.float32)
        )
        between = between + jnp.where(core == 1, rfold_ref[z, 0], 0.0)
        before = jnp.sum(between, axis=1, keepdims=True) + jnp.where(
            diagonal, 0.0, ends[heads : 2 * heads] + ends[2 * heads : 3 * heads]
        )
        arow = (scan_ref[0:heads, :] + before) * LOG2E

        @pl.loop(0, z + 1)
        def _(slot):
            @pl.when(slot != ka)
            def _():
                stat_copy(slot, slot).wait_recv()

        peaks = stat_ref[:, 0:heads, :]
        totals = stat_ref[:, heads : 2 * heads, :]
        peak = jnp.max(peaks, axis=0)
        total = jnp.sum(totals * jnp.exp2(peaks - peak[None]), axis=0)
        own_peak = stat_ref[ka, 0:heads, :]
        scaling = jnp.exp2(own_peak - peak) / total

        def grad_turn(t, row_sums):
            rows = chunk_rows(t)
            mask = mask_of(t)
            b_rows = b_ref[rows, :]
            out = jnp.zeros((CHUNK, cols), jnp.float32)
            new_sums = []
            for h in range(heads):
                inner = dot(b_rows, ch_ref[h], ((1,), (1,)))
                gap = jnp.concatenate(
                    [kcol_ref[h, rows, :]] * (qn // 128), axis=1
                ) - arow[h : h + 1, :]
                decay = jnp.exp2(jnp.where(mask, gap, NEGATIVE))
                student = inner * decay
                grad = student - s_ref[h, rows, :] * scaling[h : h + 1, :]
                weight = (grad * decay).astype(jnp.bfloat16)
                w_ref[h, rows, :] = weight
                related = grad * student
                flipped = jnp.transpose(fold_lanes(related))
                cs_ref[t, h : h + 1, :] = jnp.sum(flipped, axis=0, keepdims=True)
                new_sums.append(row_sums[h] + fold_rows(related))
                out = out + dot(weight, ch_ref[h], ((1,), (0,)))
            gbpart_ref[pl.ds(t * per_chunk, per_chunk)] = (out * factor).reshape(
                per_chunk, 2, gb_rows, cols
            )
            gx_copy(t * per_chunk, per_chunk).start()
            return tuple(new_sums)

        row_sums = lax.fori_loop(
            0,
            steps,
            grad_turn,
            tuple(jnp.zeros((8, qn), jnp.float32) for _ in range(heads)),
        )
        cs_copy().start()

        for h in range(heads):
            slope_ref[ka, h : h + 1, 0:qn] = jnp.sum(
                row_sums[h], axis=0, keepdims=True
            )
            flat = dot(
                bt_ref[h * state : (h + 1) * state, :], w_ref[h], ((1,), (0,))
            )
            gcown_ref[:, h * state : (h + 1) * state] = jnp.transpose(flat * factor)

        gcsend_ref[...] = (
            gcown_ref[...].reshape(na, gc_rows, cols).astype(jnp.bfloat16)
        )

        cs_copy().wait_recv()
        sib_fold = jnp.sum(cssib_ref[...], axis=0)
        fold_ref[z] = jnp.sum(cs_ref[...], axis=0) + sib_fold
        mine = pl.ds(core * half, half)
        colsend_ref[...] = cs_ref[mine] + cssib_ref[mine]

        @pl.when(jnp.logical_not(diagonal))
        def _():
            col_copy(z).start()

        @pl.loop(ka, z)
        def _(target):
            fold_copy(z, target).start()

        @pl.loop(1, na)
        def _(k):
            gc_copy(ka, lax.rem(ka + k, na)).start()

        gx_copy(0, nz).wait_recv()

        @pl.loop(1, nz)
        def _(k):
            target = lax.rem(z + k, nz)
            gbsend_ref[target] = (
                gbpart_ref[target, core] + gbsib_ref[target]
            ).astype(jnp.bfloat16)
            gb_copy(z, target).start()

        gbown_ref[...] = gbpart_ref[z, core] + gbsib_ref[z]

        def later_turn(slot, total):
            fold_copy(slot, z).wait_recv()
            return total + fold_ref[slot]

        later = lax.fori_loop(
            z + 1, nz, later_turn, jnp.where(core == 0, sib_fold, 0.0)
        )
        slope_ref[ka, :, qn:] = later

        @pl.when(diagonal)
        def _():
            def col_turn(slot, total):
                col_copy(slot).wait_recv()
                return total + col_ref[slot]

            above = lax.fori_loop(
                z + 1, nz, col_turn, jnp.zeros(colsend_ref.shape, jnp.float32)
            )
            everything = above + colsend_ref[...]
            for k in range(half):
                lanes = slice(k * CHUNK, (k + 1) * CHUNK)
                slope_ref[ka, :, lanes] = slope_ref[ka, :, lanes] - everything[k]

            @pl.when(core == 0)
            def _():
                slope_ref[ka, :, qn:] = jnp.sum(above + cssib_ref[mine], axis=0)

        @pl.loop(1, na)
        def _(k):
            slope_copy(ka, lax.rem(ka + k, na)).start()

    @pl.when(live)
    def _():
        gc_ref[...] = gcown_ref[
            pl.ds(pl.multiple_of(ka * gc_rows, gc_rows), gc_rows), :
        ]
        gb_ref[...] = gbown_ref[...]

    @pl.when(jnp.logical_not(live))
    def _():
        gc_ref[...] = jnp.zeros_like(gc_ref)
        gb_ref[...] = jnp.zeros_like(gb_ref)

    def gc_turn(slot, total):
        gc_copy(slot, slot).wait_recv()
        return total + gcrecv_ref[slot].astype(jnp.float32)

    sums = lax.fori_loop(0, jnp.minimum(ka, z + 1), gc_turn, gc_ref[...])
    gc_ref[...] = lax.fori_loop(ka + 1, z + 1, gc_turn, sums)

    def gb_turn(slot, total):
        gb_copy(slot, slot).wait_recv()
        return total + gbrecv_ref[slot].astype(jnp.float32)

    sums = lax.fori_loop(ka, z, gb_turn, gb_ref[...])
    gb_ref[...] = lax.fori_loop(jnp.maximum(ka, z + 1), nz, gb_turn, sums)

    @pl.when(live)
    def _():
        pair_copy(core).wait_send()
        gx_copy(0, nz).wait_send()
        cs_copy().wait_send()

        @pl.when(jnp.logical_not(diagonal))
        def _():
            col_copy(z).wait_send()

        @pl.loop(z + 1, nz)
        def _(target):
            @pl.when(diagonal)
            def _():
                krate_copy(target).wait_send()

            @pl.when(jnp.logical_not(diagonal))
            def _():
                rfold_copy(z, target).wait_send()

        @pl.loop(ka, z)
        def _(target):
            fold_copy(z, target).wait_send()

        @pl.loop(0, z + 1)
        def _(target):
            @pl.when(target != ka)
            def _():
                stat_copy(ka, target).wait_send()

        rest = pl.ds(0, na - 1)
        to(gcsend_ref.at[rest], gcrecv_ref.at[rest], gc_send, gc_recv.at[0], (pb, ka)).wait_send()
        rest = pl.ds(0, nz - 1)
        to(gbsend_ref.at[rest], gbrecv_ref.at[rest], gb_send, gb_recv.at[0], (pb, ka)).wait_send()

    def slope_turn(slot, total):
        slope_copy(slot, slot).wait_recv()
        return total + slope_ref[slot]

    @pl.when(jnp.logical_not(live))
    def _():
        slope_ref[ka] = jnp.zeros(slope_ref.shape[1:], jnp.float32)

    both = lax.fori_loop(0, jnp.minimum(ka, z + 1), slope_turn, slope_ref[ka])
    both = lax.fori_loop(ka + 1, z + 1, slope_turn, both)
    slope = both[:, 0:qn]
    after = jnp.sum(both[:, qn:], axis=1, keepdims=True)
    scan_ref[...] = jnp.zeros_like(scan_ref)
    scan_ref[0:heads, :] = slope
    suffix = jnp.sum(slope, axis=1, keepdims=True) - lane_prefix(scan_ref[...])[0:heads, :]
    gr_ref[...] = -factor * (suffix + slope + after)

    @pl.when(live)
    def _():
        rest = pl.ds(0, na - 1)
        to(slope_ref.at[rest], slope_ref.at[rest], slope_send, slope_recv.at[0], (pb, ka)).wait_send()


def body(teacher_query, teacher_key, student_c, student_b, decay_rate):
    heads = decay_rate.shape[0]
    nb = lax.axis_size("pb")
    na = lax.axis_size("ka")
    qn, width = teacher_query.shape
    kn = teacher_key.shape[0]
    cols = student_c.shape[1]
    nz = nb // 2
    steps = kn // CHUNK
    f32, bf16 = jnp.float32, jnp.bfloat16
    vmem = pl.BlockSpec(memory_space=pltpu.VMEM)
    hbm = pl.BlockSpec(memory_space=pl.ANY)
    dma = pltpu.SemaphoreType.DMA
    scan_rows = -(-heads * 3 // 8) * 8
    return pl.pallas_call(
        functools.partial(kernel, nb, na, heads),
        out_shape=(
            jax.ShapeDtypeStruct((qn // na, cols), f32),
            jax.ShapeDtypeStruct((kn // nb, cols), f32),
            jax.ShapeDtypeStruct((heads, qn), f32),
        ),
        in_specs=[hbm, hbm, hbm, hbm, hbm],
        out_specs=[vmem, vmem, vmem],
        scratch_shapes=[
            pltpu.VMEM((qn, width), bf16),
            pltpu.VMEM((kn, width), bf16),
            pltpu.VMEM((qn, cols), bf16),
            pltpu.VMEM((kn, cols), bf16),
            pltpu.VMEM((heads, qn, cols), bf16),
            pltpu.VMEM((cols, kn), bf16),
            pltpu.VMEM((heads, kn, qn), f32),
            pltpu.VMEM((heads, kn, qn), bf16),
            pltpu.VMEM((heads, kn, 128), f32),
            pltpu.VMEM((scan_rows, qn), f32),
            pltpu.VMEM((2, heads, qn), f32),
            pltpu.VMEM((2, heads, qn), f32),
            pltpu.VMEM((nz, 2, heads, 128), f32),
            pltpu.VMEM((na, 2 * heads, qn), f32),
            pltpu.VMEM((steps, heads, CHUNK), f32),
            pltpu.VMEM((steps, heads, CHUNK), f32),
            pltpu.VMEM((nz, heads, CHUNK), f32),
            pltpu.VMEM((steps // 2, heads, CHUNK), f32),
            pltpu.VMEM((nz, steps // 2, heads, CHUNK), f32),
            pltpu.VMEM((na, heads, qn + 128), f32),
            pltpu.VMEM((nz, 2, kn // nb, cols), f32),
            pltpu.VMEM((nz, kn // nb, cols), f32),
            pltpu.VMEM((kn // nb, cols), f32),
            pltpu.VMEM((nz, kn // nb, cols), bf16),
            pltpu.VMEM((nz, kn // nb, cols), bf16),
            pltpu.VMEM((qn, cols), f32),
            pltpu.VMEM((na, qn // na, cols), bf16),
            pltpu.VMEM((na, qn // na, cols), bf16),
            dma((5,)),
            dma,
            dma,
            dma((nz,)),
            dma,
            dma((nz,)),
            dma((na,)),
            dma((na,)),
            dma,
            dma,
            dma((nz,)),
            dma((nz,)),
            dma,
            dma((nz,)),
            dma,
            dma((na,)),
            dma,
            dma,
            dma,
            dma((nz,)),
            dma,
            dma((na,)),
        ],
        compiler_params=pltpu.CompilerParams(
            collective_id=0, has_side_effects=True, vmem_limit_bytes=62 * 1024 * 1024
        ),
    )(teacher_query, teacher_key, student_c, student_b, decay_rate)


def solution(mesh):
    placed = (P("pb", None), P("ka", None), P("pb", None), P("ka", None), P(None, "pb"))
    return jax.shard_map(
        body,
        mesh=mesh,
        in_specs=placed,
        out_specs=(P(("pb", "ka"), None), P(("ka", "pb"), None), P(None, "pb")),
        check_vma=False,
    )
```

```python
import functools
import math

import jax
import jax.numpy as jnp
from jax import lax
from jax.experimental import pallas as pl
from jax.experimental.pallas import tpu as pltpu
from jax.sharding import PartitionSpec as P

MESH = pl.DeviceIdType.MESH
NEGATIVE = -1e30
LOG2E = 1.0 / math.log(2.0)
CHUNK = 256
PIECE = 16


def dot(a, b, dims):
    return lax.dot_general(a, b, (dims, ((), ())), preferred_element_type=jnp.float32)


def fold_rows(x):
    return jnp.sum(x.reshape(x.shape[0] // 8, 8, x.shape[1]), axis=0)


def fold_lanes(x):
    width = x.shape[1]
    out = x[:, 0:128]
    for k in range(128, width, 128):
        out = out + x[:, k : k + 128]
    return out


def lane_prefix(x):
    width = x.shape[1]
    lane = lax.broadcasted_iota(jnp.int32, x.shape, 1)
    shift = 1
    while shift < width:
        x = x + jnp.where(lane >= shift, pltpu.roll(x, shift, 1), 0.0)
        shift *= 2
    return x


def kernel(
    nb,
    na,
    heads,
    q_hbm,
    k_hbm,
    c_hbm,
    b_hbm,
    rate_hbm,
    gc_ref,
    gb_ref,
    gr_ref,
    q_ref,
    k_ref,
    c_ref,
    b_ref,
    ch_ref,
    bt_ref,
    s_ref,
    w_ref,
    kcol_ref,
    scan_ref,
    pair_ref,
    krate_ref,
    rfold_ref,
    stat_ref,
    cs_ref,
    cssib_ref,
    fold_ref,
    colsend_ref,
    col_ref,
    slope_ref,
    rs_ref,
    gct_ref,
    gbpart_ref,
    gbsib_ref,
    gbown_ref,
    gbsend_ref,
    gbrecv_ref,
    gcown_ref,
    gcsend_ref,
    gcrecv_ref,
    in_sem,
    pair_send,
    pair_recv,
    rate_send,
    krate_recv,
    rfold_recv,
    stat_send,
    stat_recv,
    cs_send,
    cs_recv,
    fold_send,
    fold_recv,
    col_send,
    col_recv,
    slope_send,
    slope_recv,
    gx_send,
    gx_recv,
    gb_send,
    gb_recv,
    gc_send,
    gc_recv,
):
    pb = lax.axis_index("pb")
    ka = lax.axis_index("ka")
    qn, width = q_ref.shape
    kn = k_ref.shape[0]
    dh = width // heads
    cols = c_ref.shape[1]
    state = cols // heads
    nz = nb // 2
    z = pb // 2
    core = lax.rem(pb, 2)
    other = 1 - core
    sibling = 2 * z + other
    steps = kn // CHUNK
    half = qn // 128
    pieces = CHUNK // PIECE
    blocks = CHUNK // 128
    gb_rows = kn // nb
    gc_rows = qn // na
    per_chunk = CHUNK // (2 * gb_rows)
    factor = 2.0 * qn * nb
    live = z >= ka
    diagonal = z == ka

    loads = [
        pltpu.make_async_copy(src, dst, in_sem.at[n])
        for n, (src, dst) in enumerate(
            (
                (q_hbm, q_ref),
                (k_hbm, k_ref),
                (rate_hbm, pair_ref.at[core]),
                (c_hbm, c_ref),
                (b_hbm, b_ref),
            )
        )
    ]
    for load in loads:
        load.start()

    barrier = pltpu.get_barrier_semaphore()
    pl.semaphore_signal(barrier, inc=1, device_id=(sibling, ka), device_id_type=MESH)

    @pl.loop(1, na)
    def _(k):
        pl.semaphore_signal(
            barrier, inc=1, device_id=(pb, lax.rem(ka + k, na)), device_id_type=MESH
        )

    @pl.loop(1, nz)
    def _(k):
        pl.semaphore_signal(
            barrier,
            inc=1,
            device_id=(2 * lax.rem(z + k, nz) + core, ka),
            device_id_type=MESH,
        )

    def to(src, dst, send, recv, device):
        return pltpu.make_async_remote_copy(
            src_ref=src,
            dst_ref=dst,
            send_sem=send,
            recv_sem=recv,
            device_id=device,
            device_id_type=MESH,
        )

    def up(target):
        return (2 * target + core, ka)

    def pair_copy(slot):
        return to(
            pair_ref.at[slot], pair_ref.at[slot], pair_send, pair_recv, (sibling, ka)
        )

    def krate_copy(target):
        return to(pair_ref, krate_ref, rate_send.at[target], krate_recv, up(target))

    def rfold_copy(slot, target):
        return to(
            rfold_ref.at[slot],
            rfold_ref.at[slot],
            rate_send.at[target],
            rfold_recv.at[slot],
            up(target),
        )

    def stat_copy(slot, target):
        return to(
            stat_ref.at[slot],
            stat_ref.at[slot],
            stat_send.at[target],
            stat_recv.at[slot],
            (pb, target),
        )

    def cs_copy():
        return to(cs_ref, cssib_ref, cs_send, cs_recv, (sibling, ka))

    def fold_copy(slot, target):
        return to(
            fold_ref.at[slot],
            fold_ref.at[slot],
            fold_send.at[target],
            fold_recv.at[slot],
            up(target),
        )

    def col_copy(slot):
        return to(
            colsend_ref, col_ref.at[slot], col_send, col_recv.at[slot], up(ka)
        )

    def slope_copy(slot, target):
        return to(
            slope_ref.at[slot],
            slope_ref.at[slot],
            slope_send,
            slope_recv.at[slot],
            (pb, target),
        )

    def gx_copy(start, count):
        return to(
            gbpart_ref.at[pl.ds(start, count), other],
            gbsib_ref.at[pl.ds(start, count)],
            gx_send,
            gx_recv.at[start // per_chunk],
            (sibling, ka),
        )

    def gb_copy(slot, target):
        return to(
            gbsend_ref.at[target],
            gbrecv_ref.at[slot],
            gb_send,
            gb_recv.at[slot],
            up(target),
        )

    def gc_copy(slot, target):
        return to(
            gcsend_ref.at[target],
            gcrecv_ref.at[slot],
            gc_send,
            gc_recv.at[slot],
            (pb, target),
        )

    offset = pb * qn - ka * kn

    def mask_of(t, piece):
        rows = lax.broadcasted_iota(jnp.int32, (PIECE, qn), 0)
        lanes = lax.broadcasted_iota(jnp.int32, (PIECE, qn), 1)
        return lanes - rows >= t * CHUNK + piece * PIECE - offset

    def piece_rows(t, piece):
        return pl.ds(pl.multiple_of(t * CHUNK + piece * PIECE, PIECE), PIECE)

    def chunk_rows(t):
        return pl.ds(pl.multiple_of(t * CHUNK, CHUNK), CHUNK)

    scale2 = LOG2E / math.sqrt(dh)

    def head_stats(h, masked):
        lanes = slice(h * dh, (h + 1) * dh)

        def score_turn(t, peak):
            s = dot(k_ref[chunk_rows(t), lanes], q_ref[:, lanes], ((1,), (1,)))
            for n in range(pieces):
                part = s[n * PIECE : (n + 1) * PIECE] * scale2
                if masked:
                    part = jnp.where(mask_of(t, n), part, NEGATIVE)
                s_ref[h, piece_rows(t, n), :] = part
                for k in range(0, PIECE, 8):
                    peak = jnp.maximum(peak, part[k : k + 8])
            return peak

        peak = lax.fori_loop(
            0, steps, score_turn, jnp.full((8, qn), NEGATIVE, jnp.float32)
        )
        peak = jnp.max(peak, axis=0, keepdims=True)

        def expo_turn(t, total):
            for n in range(pieces):
                e = jnp.exp2(s_ref[h, piece_rows(t, n), :] - peak)
                s_ref[h, piece_rows(t, n), :] = e
                for k in range(0, PIECE, 8):
                    total = total + e[k : k + 8]
            return total

        total = lax.fori_loop(0, steps, expo_turn, jnp.zeros((8, qn), jnp.float32))
        stat_ref[ka, h : h + 1, :] = peak
        stat_ref[ka, heads + h : heads + h + 1, :] = jnp.sum(
            total, axis=0, keepdims=True
        )

    def stats(first, last):
        @pl.when(diagonal)
        def _():
            for h in range(first, last):
                head_stats(h, True)

        @pl.when(z > ka)
        def _():
            for h in range(first, last):
                head_stats(h, False)

    @pl.when(live)
    def _():
        stat_init = jnp.concatenate(
            [
                jnp.full((heads, qn), NEGATIVE, jnp.float32),
                jnp.zeros((heads, qn), jnp.float32),
            ],
            axis=0,
        )

        @pl.loop(z + 1, na)
        def _(slot):
            stat_ref[slot] = stat_init

    loads[0].wait()
    loads[1].wait()

    stats(0, heads // 2)

    for load in loads[2:]:
        load.wait()
    pl.semaphore_wait(barrier, na + nz - 1)

    @pl.when(live)
    def _():
        pair_copy(core).start()
        stats(heads // 2, heads)

        @pl.loop(1, na)
        def _(k):
            target = lax.rem(ka + k, na)

            @pl.when(target <= z)
            def _():
                stat_copy(ka, target).start()

        pair_copy(other).wait_recv()
        own_fold = jnp.stack([fold_lanes(pair_ref[0]), fold_lanes(pair_ref[1])])
        rfold_ref[z] = own_fold

        @pl.loop(z + 1, nz)
        def _(target):
            @pl.when(diagonal)
            def _():
                krate_copy(target).start()

            @pl.when(jnp.logical_not(diagonal))
            def _():
                rfold_copy(z, target).start()

        head_of = lax.broadcasted_iota(jnp.int32, (qn, cols), 1) // state
        c_all = c_ref[...]
        for h in range(heads):
            ch_ref[h] = jnp.where(head_of == h, c_all, jnp.zeros_like(c_all))
        for t in range(steps):
            bt_ref[t] = jnp.transpose(b_ref[t * CHUNK : (t + 1) * CHUNK, :])

        scan_ref[...] = jnp.zeros_like(scan_ref)
        scan_ref[0:heads, :] = pair_ref[core]

        @pl.when(diagonal)
        def _():
            for part in range(2):
                low = heads * (1 + part)
                scan_ref[low : low + heads, :] = pair_ref[part]

        @pl.when(jnp.logical_not(diagonal))
        def _():
            krate_copy(z).wait_recv()
            for part in range(2):
                low = heads * (1 + part)
                scan_ref[low : low + heads, :] = krate_ref[part]

        rates = scan_ref[...]
        scan_ref[...] = lane_prefix(rates)
        ends = jnp.sum(rates, axis=1, keepdims=True)
        for h in range(heads):
            shift = jnp.zeros((1, 1), jnp.float32)
            for part in range(2):
                row = heads * (1 + part) + h
                prefix = (scan_ref[row : row + 1, :] + shift) * LOG2E
                kcol_ref[h, part * qn : (part + 1) * qn, :] = jnp.transpose(
                    jnp.broadcast_to(prefix, (128, qn))
                )
                shift = shift + ends[row : row + 1, :]

        def between_turn(slot, total):
            rfold_copy(slot, z).wait_recv()
            return total + rfold_ref[slot, 0] + rfold_ref[slot, 1]

        between = lax.fori_loop(
            ka + 1, z, between_turn, jnp.zeros((heads, 128), jnp.float32)
        )
        between = between + jnp.where(core == 1, rfold_ref[z, 0], 0.0)
        before = jnp.sum(between, axis=1, keepdims=True) + jnp.where(
            diagonal, 0.0, ends[heads : 2 * heads] + ends[2 * heads : 3 * heads]
        )
        arow = (scan_ref[0:heads, :] + before) * LOG2E

        @pl.loop(0, z + 1)
        def _(slot):
            @pl.when(slot != ka)
            def _():
                stat_copy(slot, slot).wait_recv()

        peaks = stat_ref[:, 0:heads, :]
        totals = stat_ref[:, heads : 2 * heads, :]
        peak = jnp.max(peaks, axis=0)
        total = jnp.sum(totals * jnp.exp2(peaks - peak[None]), axis=0)
        own_peak = stat_ref[ka, 0:heads, :]
        scaling = jnp.exp2(own_peak - peak) / total

        def send_grad_b(t):
            gx_copy(t * per_chunk, per_chunk).wait_recv()

            @pl.loop(0, per_chunk)
            def _(k):
                target = t * per_chunk + k
                sums = gbpart_ref[target, core] + gbsib_ref[target]

                @pl.when(target == z)
                def _():
                    gbown_ref[...] = sums

                @pl.when(target != z)
                def _():
                    gbsend_ref[target] = sums.astype(jnp.bfloat16)
                    gb_copy(z, target).start()

        def turn_chunk(n):
            return lax.rem(n + z // per_chunk, steps)

        def grad_pass(masked):
            def grad_turn(n, row_sums):
                t = turn_chunk(n)
                rows = chunk_rows(t)
                b_rows = b_ref[rows, :]
                inners = [dot(b_rows, ch_ref[h], ((1,), (1,))) for h in range(heads)]
                out = jnp.zeros((CHUNK, cols), jnp.float32)
                new_sums = []
                for h in range(heads):
                    sums = row_sums[h]
                    weights = []
                    folds = []
                    for m in range(pieces):
                        at = piece_rows(t, m)
                        column = kcol_ref[h, at, :]
                        gap = (
                            jnp.concatenate([column] * (qn // 128), axis=1)
                            - arow[h : h + 1, :]
                        )
                        if masked:
                            gap = jnp.where(mask_of(t, m), gap, NEGATIVE)
                        decay = jnp.exp2(gap)
                        student = inners[h][m * PIECE : (m + 1) * PIECE] * decay
                        grad = student - s_ref[h, at, :] * scaling[h : h + 1, :]
                        weights.append((grad * decay).astype(jnp.bfloat16))
                        related = grad * student
                        folds.append(fold_lanes(related))
                        for k in range(0, PIECE, 8):
                            sums = sums + related[k : k + 8]
                    new_sums.append(sums)
                    weight = jnp.concatenate(weights, axis=0)
                    out = out + dot(weight, ch_ref[h], ((1,), (0,)))
                    low = slice(h * state, (h + 1) * state)
                    turned = bt_ref[t, low, :]
                    gct_ref[low, :] += dot(turned, weight, ((1,), (0,)))
                    fold = jnp.concatenate(folds, axis=0)
                    for k in range(blocks):
                        flipped = jnp.transpose(fold[k * 128 : (k + 1) * 128])
                        cs_ref[t * blocks + k, h : h + 1, :] = jnp.sum(
                            flipped, axis=0, keepdims=True
                        )
                gbpart_ref[pl.ds(t * per_chunk, per_chunk)] = (out * factor).reshape(
                    per_chunk, 2, gb_rows, cols
                )
                gx_copy(t * per_chunk, per_chunk).start()

                @pl.when(n > 0)
                def _():
                    send_grad_b(turn_chunk(n - 1))

                return tuple(new_sums)

            row_sums = lax.fori_loop(
                0,
                steps,
                grad_turn,
                tuple(jnp.zeros((8, qn), jnp.float32) for _ in range(heads)),
            )
            for h in range(heads):
                rs_ref[h] = row_sums[h]

        gct_ref[...] = jnp.zeros_like(gct_ref)

        @pl.when(diagonal)
        def _():
            grad_pass(True)

        @pl.when(z > ka)
        def _():
            grad_pass(False)

        cs_copy().start()

        for h in range(heads):
            slope_ref[ka, h : h + 1, 0:qn] = jnp.sum(rs_ref[h], axis=0, keepdims=True)
        gcown_ref[...] = jnp.transpose(gct_ref[...] * factor)
        gcsend_ref[...] = (
            gcown_ref[...].reshape(na, gc_rows, cols).astype(jnp.bfloat16)
        )

        cs_copy().wait_recv()
        sib_fold = jnp.sum(cssib_ref[...], axis=0)
        fold_ref[z] = jnp.sum(cs_ref[...], axis=0) + sib_fold
        mine = pl.ds(core * half, half)
        colsend_ref[...] = cs_ref[mine] + cssib_ref[mine]

        @pl.when(jnp.logical_not(diagonal))
        def _():
            col_copy(z).start()

        @pl.loop(ka, z)
        def _(target):
            fold_copy(z, target).start()

        @pl.loop(1, na)
        def _(k):
            gc_copy(ka, lax.rem(ka + k, na)).start()

        send_grad_b(turn_chunk(steps - 1))

        def later_turn(slot, total):
            fold_copy(slot, z).wait_recv()
            return total + fold_ref[slot]

        later = lax.fori_loop(
            z + 1, nz, later_turn, jnp.where(core == 0, sib_fold, 0.0)
        )
        slope_ref[ka, :, qn:] = later

        @pl.when(diagonal)
        def _():
            def col_turn(slot, total):
                col_copy(slot).wait_recv()
                return total + col_ref[slot]

            above = lax.fori_loop(
                z + 1, nz, col_turn, jnp.zeros(colsend_ref.shape, jnp.float32)
            )
            everything = above + colsend_ref[...]
            for k in range(half):
                lanes = slice(k * 128, (k + 1) * 128)
                slope_ref[ka, :, lanes] = slope_ref[ka, :, lanes] - everything[k]

            @pl.when(core == 0)
            def _():
                slope_ref[ka, :, qn:] = jnp.sum(above + cssib_ref[mine], axis=0)

        @pl.loop(1, na)
        def _(k):
            slope_copy(ka, lax.rem(ka + k, na)).start()

    @pl.when(live)
    def _():
        gc_ref[...] = gcown_ref[
            pl.ds(pl.multiple_of(ka * gc_rows, gc_rows), gc_rows), :
        ]
        gb_ref[...] = gbown_ref[...]

    @pl.when(jnp.logical_not(live))
    def _():
        gc_ref[...] = jnp.zeros_like(gc_ref)
        gb_ref[...] = jnp.zeros_like(gb_ref)

    def gc_turn(slot, total):
        gc_copy(slot, slot).wait_recv()
        return total + gcrecv_ref[slot].astype(jnp.float32)

    sums = lax.fori_loop(0, jnp.minimum(ka, z + 1), gc_turn, gc_ref[...])
    gc_ref[...] = lax.fori_loop(ka + 1, z + 1, gc_turn, sums)

    def gb_turn(slot, total):
        gb_copy(slot, slot).wait_recv()
        return total + gbrecv_ref[slot].astype(jnp.float32)

    sums = lax.fori_loop(ka, z, gb_turn, gb_ref[...])
    gb_ref[...] = lax.fori_loop(jnp.maximum(ka, z + 1), nz, gb_turn, sums)

    @pl.when(live)
    def _():
        pair_copy(core).wait_send()
        to(
            gbpart_ref.at[pl.ds(0, nz), other], gbsib_ref, gx_send, gx_recv.at[0], (sibling, ka)
        ).wait_send()
        cs_copy().wait_send()

        @pl.when(jnp.logical_not(diagonal))
        def _():
            col_copy(z).wait_send()

        @pl.loop(z + 1, nz)
        def _(target):
            @pl.when(diagonal)
            def _():
                krate_copy(target).wait_send()

            @pl.when(jnp.logical_not(diagonal))
            def _():
                rfold_copy(z, target).wait_send()

        @pl.loop(ka, z)
        def _(target):
            fold_copy(z, target).wait_send()

        @pl.loop(0, z + 1)
        def _(target):
            @pl.when(target != ka)
            def _():
                stat_copy(ka, target).wait_send()

        rest = pl.ds(0, na - 1)
        to(gcsend_ref.at[rest], gcrecv_ref.at[rest], gc_send, gc_recv.at[0], (pb, ka)).wait_send()
        rest = pl.ds(0, nz - 1)
        to(gbsend_ref.at[rest], gbrecv_ref.at[rest], gb_send, gb_recv.at[0], (pb, ka)).wait_send()

    def slope_turn(slot, total):
        slope_copy(slot, slot).wait_recv()
        return total + slope_ref[slot]

    @pl.when(jnp.logical_not(live))
    def _():
        slope_ref[ka] = jnp.zeros(slope_ref.shape[1:], jnp.float32)

    both = lax.fori_loop(0, jnp.minimum(ka, z + 1), slope_turn, slope_ref[ka])
    both = lax.fori_loop(ka + 1, z + 1, slope_turn, both)
    slope = both[:, 0:qn]
    after = jnp.sum(both[:, qn:], axis=1, keepdims=True)
    scan_ref[...] = jnp.zeros_like(scan_ref)
    scan_ref[0:heads, :] = slope
    suffix = jnp.sum(slope, axis=1, keepdims=True) - lane_prefix(scan_ref[...])[0:heads, :]
    gr_ref[...] = -factor * (suffix + slope + after)

    @pl.when(live)
    def _():
        rest = pl.ds(0, na - 1)
        to(slope_ref.at[rest], slope_ref.at[rest], slope_send, slope_recv.at[0], (pb, ka)).wait_send()


def place(gc_in, gb_in, gr_in, gc_out, gb_out, gr_out, sem):
    copies = [
        pltpu.make_async_copy(src, dst, sem.at[n])
        for n, (src, dst) in enumerate(
            ((gc_in, gc_out), (gb_in, gb_out), (gr_in, gr_out))
        )
    ]
    for copy in copies:
        copy.start()
    for copy in copies:
        copy.wait()


def body(teacher_query, teacher_key, student_c, student_b, decay_rate):
    heads = decay_rate.shape[0]
    nb = lax.axis_size("pb")
    na = lax.axis_size("ka")
    qn, width = teacher_query.shape
    kn = teacher_key.shape[0]
    cols = student_c.shape[1]
    nz = nb // 2
    steps = kn // CHUNK
    f32, bf16 = jnp.float32, jnp.bfloat16
    vmem = pl.BlockSpec(memory_space=pltpu.VMEM)
    hbm = pl.BlockSpec(memory_space=pl.ANY)
    dma = pltpu.SemaphoreType.DMA
    scan_rows = -(-heads * 3 // 8) * 8
    shapes = (
        jax.ShapeDtypeStruct((qn // na, cols), f32),
        jax.ShapeDtypeStruct((kn // nb, cols), f32),
        jax.ShapeDtypeStruct((heads, qn), f32),
    )
    results = pl.pallas_call(
        functools.partial(kernel, nb, na, heads),
        out_shape=shapes,
        in_specs=[hbm, hbm, hbm, hbm, hbm],
        out_specs=[vmem, vmem, vmem],
        scratch_shapes=[
            pltpu.VMEM((qn, width), bf16),
            pltpu.VMEM((kn, width), bf16),
            pltpu.VMEM((qn, cols), bf16),
            pltpu.VMEM((kn, cols), bf16),
            pltpu.VMEM((heads, qn, cols), bf16),
            pltpu.VMEM((steps, cols, CHUNK), bf16),
            pltpu.VMEM((heads, kn, qn), f32),
            pltpu.VMEM((heads, kn, qn), bf16),
            pltpu.VMEM((heads, kn, 128), f32),
            pltpu.VMEM((scan_rows, qn), f32),
            pltpu.VMEM((2, heads, qn), f32),
            pltpu.VMEM((2, heads, qn), f32),
            pltpu.VMEM((nz, 2, heads, 128), f32),
            pltpu.VMEM((na, 2 * heads, qn), f32),
            pltpu.VMEM((kn // 128, heads, 128), f32),
            pltpu.VMEM((kn // 128, heads, 128), f32),
            pltpu.VMEM((nz, heads, 128), f32),
            pltpu.VMEM((qn // 128, heads, 128), f32),
            pltpu.VMEM((nz, qn // 128, heads, 128), f32),
            pltpu.VMEM((na, heads, qn + 128), f32),
            pltpu.VMEM((heads, 8, qn), f32),
            pltpu.VMEM((cols, qn), f32),
            pltpu.VMEM((nz, 2, kn // nb, cols), f32),
            pltpu.VMEM((nz, kn // nb, cols), f32),
            pltpu.VMEM((kn // nb, cols), f32),
            pltpu.VMEM((nz, kn // nb, cols), bf16),
            pltpu.VMEM((nz, kn // nb, cols), bf16),
            pltpu.VMEM((qn, cols), f32),
            pltpu.VMEM((na, qn // na, cols), bf16),
            pltpu.VMEM((na, qn // na, cols), bf16),
            dma((5,)),
            dma,
            dma,
            dma((nz,)),
            dma,
            dma((nz,)),
            dma((na,)),
            dma((na,)),
            dma,
            dma,
            dma((nz,)),
            dma((nz,)),
            dma,
            dma((nz,)),
            dma,
            dma((na,)),
            dma,
            dma((steps,)),
            dma,
            dma((nz,)),
            dma,
            dma((na,)),
        ],
        compiler_params=pltpu.CompilerParams(
            collective_id=0, has_side_effects=True, vmem_limit_bytes=62 * 1024 * 1024
        ),
    )(teacher_query, teacher_key, student_c, student_b, decay_rate)
    return pl.pallas_call(
        place,
        out_shape=shapes,
        in_specs=[hbm, hbm, hbm],
        out_specs=[hbm, hbm, hbm],
        scratch_shapes=[dma((3,))],
        compiler_params=pltpu.CompilerParams(vmem_limit_bytes=62 * 1024 * 1024),
    )(*results)


def solution(mesh):
    placed = (P("pb", None), P("ka", None), P("pb", None), P("ka", None), P(None, "pb"))
    return jax.shard_map(
        body,
        mesh=mesh,
        in_specs=placed,
        out_specs=(P(("pb", "ka"), None), P(("ka", "pb"), None), P(None, "pb")),
        check_vma=False,
    )
```

```python
import functools
import math

import jax
import jax.numpy as jnp
from jax import lax
from jax.experimental import pallas as pl
from jax.experimental.pallas import tpu as pltpu
from jax.sharding import PartitionSpec as P

MESH = pl.DeviceIdType.MESH
NEGATIVE = -1e30
LOG2E = 1.0 / math.log(2.0)
CHUNK = 256
PIECE = 16


def dot(a, b, dims):
    return lax.dot_general(a, b, (dims, ((), ())), preferred_element_type=jnp.float32)


def fold_rows(x):
    return jnp.sum(x.reshape(x.shape[0] // 8, 8, x.shape[1]), axis=0)


def fold_lanes(x):
    width = x.shape[1]
    out = x[:, 0:128]
    for k in range(128, width, 128):
        out = out + x[:, k : k + 128]
    return out


def lane_prefix(x):
    width = x.shape[1]
    lane = lax.broadcasted_iota(jnp.int32, x.shape, 1)
    shift = 1
    while shift < width:
        x = x + jnp.where(lane >= shift, pltpu.roll(x, shift, 1), 0.0)
        shift *= 2
    return x


def kernel(
    nb,
    na,
    heads,
    q_hbm,
    k_hbm,
    c_hbm,
    b_hbm,
    rate_hbm,
    gc_ref,
    gb_ref,
    gr_ref,
    q_ref,
    k_ref,
    c_ref,
    b_ref,
    ch_ref,
    bt_ref,
    s_ref,
    st_ref,
    dec_ref,
    w_ref,
    kcol_ref,
    scan_ref,
    pair_ref,
    krate_ref,
    rfold_ref,
    stat_ref,
    cs_ref,
    cssib_ref,
    fold_ref,
    colsend_ref,
    col_ref,
    slope_ref,
    rs_ref,
    gbpart_ref,
    gbsib_ref,
    gbown_ref,
    gbsend_ref,
    gbrecv_ref,
    gcown_ref,
    gcsend_ref,
    gcrecv_ref,
    in_sem,
    pair_send,
    pair_recv,
    rate_send,
    krate_recv,
    rfold_recv,
    stat_send,
    stat_recv,
    cs_send,
    cs_recv,
    fold_send,
    fold_recv,
    col_send,
    col_recv,
    slope_send,
    slope_recv,
    gx_send,
    gx_recv,
    gb_send,
    gb_recv,
    gc_send,
    gc_recv,
):
    pb = lax.axis_index("pb")
    ka = lax.axis_index("ka")
    qn, width = q_ref.shape
    kn = k_ref.shape[0]
    dh = width // heads
    cols = c_ref.shape[1]
    state = cols // heads
    nz = nb // 2
    z = pb // 2
    core = lax.rem(pb, 2)
    other = 1 - core
    sibling = 2 * z + other
    steps = kn // CHUNK
    half = qn // 128
    pieces = CHUNK // PIECE
    blocks = CHUNK // 128
    gb_rows = kn // nb
    gc_rows = qn // na
    per_chunk = CHUNK // (2 * gb_rows)
    factor = 2.0 * qn * nb
    live = z >= ka
    diagonal = z == ka

    loads = [
        pltpu.make_async_copy(src, dst, in_sem.at[n])
        for n, (src, dst) in enumerate(
            (
                (q_hbm, q_ref),
                (k_hbm, k_ref),
                (rate_hbm, pair_ref.at[core]),
                (c_hbm, c_ref),
                (b_hbm, b_ref),
            )
        )
    ]
    for load in loads:
        load.start()

    barrier = pltpu.get_barrier_semaphore()
    pl.semaphore_signal(barrier, inc=1, device_id=(sibling, ka), device_id_type=MESH)

    @pl.loop(1, na)
    def _(k):
        pl.semaphore_signal(
            barrier, inc=1, device_id=(pb, lax.rem(ka + k, na)), device_id_type=MESH
        )

    @pl.loop(1, nz)
    def _(k):
        pl.semaphore_signal(
            barrier,
            inc=1,
            device_id=(2 * lax.rem(z + k, nz) + core, ka),
            device_id_type=MESH,
        )

    def to(src, dst, send, recv, device):
        return pltpu.make_async_remote_copy(
            src_ref=src,
            dst_ref=dst,
            send_sem=send,
            recv_sem=recv,
            device_id=device,
            device_id_type=MESH,
        )

    def up(target):
        return (2 * target + core, ka)

    def pair_copy(slot):
        return to(
            pair_ref.at[slot], pair_ref.at[slot], pair_send, pair_recv, (sibling, ka)
        )

    def krate_copy(target):
        return to(pair_ref, krate_ref, rate_send.at[target], krate_recv, up(target))

    def rfold_copy(slot, target):
        return to(
            rfold_ref.at[slot],
            rfold_ref.at[slot],
            rate_send.at[target],
            rfold_recv.at[slot],
            up(target),
        )

    def stat_copy(slot, target):
        return to(
            stat_ref.at[slot],
            stat_ref.at[slot],
            stat_send.at[target],
            stat_recv.at[slot],
            (pb, target),
        )

    def cs_copy():
        return to(cs_ref, cssib_ref, cs_send, cs_recv, (sibling, ka))

    def fold_copy(slot, target):
        return to(
            fold_ref.at[slot],
            fold_ref.at[slot],
            fold_send.at[target],
            fold_recv.at[slot],
            up(target),
        )

    def col_copy(slot):
        return to(
            colsend_ref, col_ref.at[slot], col_send, col_recv.at[slot], up(ka)
        )

    def slope_copy(slot, target):
        return to(
            slope_ref.at[slot],
            slope_ref.at[slot],
            slope_send,
            slope_recv.at[slot],
            (pb, target),
        )

    def gx_copy(start, count):
        return to(
            gbpart_ref.at[pl.ds(start, count), other],
            gbsib_ref.at[pl.ds(start, count)],
            gx_send,
            gx_recv.at[start // per_chunk],
            (sibling, ka),
        )

    def gb_copy(slot, target):
        return to(
            gbsend_ref.at[target],
            gbrecv_ref.at[slot],
            gb_send,
            gb_recv.at[slot],
            up(target),
        )

    def gc_copy(slot, target):
        return to(
            gcsend_ref.at[target],
            gcrecv_ref.at[slot],
            gc_send,
            gc_recv.at[slot],
            (pb, target),
        )

    offset = pb * qn - ka * kn

    def mask_of(t, piece):
        rows = lax.broadcasted_iota(jnp.int32, (PIECE, qn), 0)
        lanes = lax.broadcasted_iota(jnp.int32, (PIECE, qn), 1)
        return lanes - rows >= t * CHUNK + piece * PIECE - offset

    def piece_rows(t, piece):
        return pl.ds(pl.multiple_of(t * CHUNK + piece * PIECE, PIECE), PIECE)

    def chunk_rows(t):
        return pl.ds(pl.multiple_of(t * CHUNK, CHUNK), CHUNK)

    scale2 = LOG2E / math.sqrt(dh)

    def head_stats(h, masked):
        lanes = slice(h * dh, (h + 1) * dh)

        def score_turn(t, peak):
            s = dot(k_ref[chunk_rows(t), lanes], q_ref[:, lanes], ((1,), (1,)))
            for n in range(pieces):
                part = s[n * PIECE : (n + 1) * PIECE] * scale2
                if masked:
                    part = jnp.where(mask_of(t, n), part, NEGATIVE)
                s_ref[h, piece_rows(t, n), :] = part
                for k in range(0, PIECE, 8):
                    peak = jnp.maximum(peak, part[k : k + 8])
            return peak

        peak = lax.fori_loop(
            0, steps, score_turn, jnp.full((8, qn), NEGATIVE, jnp.float32)
        )
        peak = jnp.max(peak, axis=0, keepdims=True)

        def expo_turn(t, total):
            for n in range(pieces):
                e = jnp.exp2(s_ref[h, piece_rows(t, n), :] - peak)
                s_ref[h, piece_rows(t, n), :] = e
                for k in range(0, PIECE, 8):
                    total = total + e[k : k + 8]
            return total

        total = lax.fori_loop(0, steps, expo_turn, jnp.zeros((8, qn), jnp.float32))
        stat_ref[ka, h : h + 1, :] = peak
        stat_ref[ka, heads + h : heads + h + 1, :] = jnp.sum(
            total, axis=0, keepdims=True
        )

    def stats(first, last):
        @pl.when(diagonal)
        def _():
            for h in range(first, last):
                head_stats(h, True)

        @pl.when(z > ka)
        def _():
            for h in range(first, last):
                head_stats(h, False)

    @pl.when(live)
    def _():
        stat_init = jnp.concatenate(
            [
                jnp.full((heads, qn), NEGATIVE, jnp.float32),
                jnp.zeros((heads, qn), jnp.float32),
            ],
            axis=0,
        )

        @pl.loop(z + 1, na)
        def _(slot):
            stat_ref[slot] = stat_init

    loads[0].wait()
    loads[1].wait()

    stats(0, heads // 2)

    for load in loads[2:]:
        load.wait()
    pl.semaphore_wait(barrier, na + nz - 1)

    @pl.when(live)
    def _():
        pair_copy(core).start()
        stats(heads // 2, heads)

        pair_copy(other).wait_recv()
        own_fold = jnp.stack([fold_lanes(pair_ref[0]), fold_lanes(pair_ref[1])])
        rfold_ref[z] = own_fold

        @pl.loop(z + 1, nz)
        def _(target):
            @pl.when(diagonal)
            def _():
                krate_copy(target).start()

            @pl.when(jnp.logical_not(diagonal))
            def _():
                rfold_copy(z, target).start()

        @pl.loop(1, na)
        def _(k):
            target = lax.rem(ka + k, na)

            @pl.when(target <= z)
            def _():
                stat_copy(ka, target).start()

        head_of = lax.broadcasted_iota(jnp.int32, (qn, cols), 1) // state
        c_all = c_ref[...]
        for h in range(heads):
            ch_ref[h] = jnp.where(head_of == h, c_all, jnp.zeros_like(c_all))
        bt_ref[...] = jnp.transpose(b_ref[...])

        scan_ref[...] = jnp.zeros_like(scan_ref)
        scan_ref[0:heads, :] = pair_ref[core]

        @pl.when(diagonal)
        def _():
            for part in range(2):
                low = heads * (1 + part)
                scan_ref[low : low + heads, :] = pair_ref[part]

        @pl.when(jnp.logical_not(diagonal))
        def _():
            krate_copy(z).wait_recv()
            for part in range(2):
                low = heads * (1 + part)
                scan_ref[low : low + heads, :] = krate_ref[part]

        rates = scan_ref[...]
        scan_ref[...] = lane_prefix(rates)
        ends = jnp.sum(rates, axis=1, keepdims=True)
        for h in range(heads):
            shift = jnp.zeros((1, 1), jnp.float32)
            for part in range(2):
                row = heads * (1 + part) + h
                prefix = (scan_ref[row : row + 1, :] + shift) * LOG2E
                kcol_ref[h, part * qn : (part + 1) * qn, :] = jnp.transpose(
                    jnp.broadcast_to(prefix, (128, qn))
                )
                shift = shift + ends[row : row + 1, :]

        def between_turn(slot, total):
            rfold_copy(slot, z).wait_recv()
            return total + rfold_ref[slot, 0] + rfold_ref[slot, 1]

        between = lax.fori_loop(
            ka + 1, z, between_turn, jnp.zeros((heads, 128), jnp.float32)
        )
        between = between + jnp.where(core == 1, rfold_ref[z, 0], 0.0)
        before = jnp.sum(between, axis=1, keepdims=True) + jnp.where(
            diagonal, 0.0, ends[heads : 2 * heads] + ends[2 * heads : 3 * heads]
        )
        arow = (scan_ref[0:heads, :] + before) * LOG2E

        def student_pass(masked):
            def student_turn(t, sums):
                b_rows = b_ref[chunk_rows(t), :]
                inners = [dot(b_rows, ch_ref[h], ((1,), (1,))) for h in range(heads)]
                new_sums = []
                for h in range(heads):
                    squares, mixed = sums[h]
                    for m in range(pieces):
                        at = piece_rows(t, m)
                        column = kcol_ref[h, at, :]
                        gap = (
                            jnp.concatenate([column] * (qn // 128), axis=1)
                            - arow[h : h + 1, :]
                        )
                        if masked:
                            gap = jnp.where(mask_of(t, m), gap, NEGATIVE)
                        decay = jnp.exp2(gap)
                        student = inners[h][m * PIECE : (m + 1) * PIECE] * decay
                        dec_ref[h, at, :] = decay
                        st_ref[h, at, :] = student
                        square = student * student
                        mix = student * s_ref[h, at, :]
                        for k in range(0, PIECE, 8):
                            squares = squares + square[k : k + 8]
                            mixed = mixed + mix[k : k + 8]
                    new_sums.append((squares, mixed))
                return tuple(new_sums)

            zero = jnp.zeros((8, qn), jnp.float32)
            sums = lax.fori_loop(
                0, steps, student_turn, tuple((zero, zero) for _ in range(heads))
            )
            for h in range(heads):
                rs_ref[h, 0] = sums[h][0]
                rs_ref[h, 1] = sums[h][1]

        @pl.when(diagonal)
        def _():
            student_pass(True)

        @pl.when(z > ka)
        def _():
            student_pass(False)

        @pl.loop(0, z + 1)
        def _(slot):
            @pl.when(slot != ka)
            def _():
                stat_copy(slot, slot).wait_recv()

        peaks = stat_ref[:, 0:heads, :]
        totals = stat_ref[:, heads : 2 * heads, :]
        peak = jnp.max(peaks, axis=0)
        total = jnp.sum(totals * jnp.exp2(peaks - peak[None]), axis=0)
        own_peak = stat_ref[ka, 0:heads, :]
        scaling = jnp.exp2(own_peak - peak) / total

        def send_grad_b(t):
            gx_copy(t * per_chunk, per_chunk).wait_recv()

            @pl.loop(0, per_chunk)
            def _(k):
                target = t * per_chunk + k
                sums = gbpart_ref[target, core] + gbsib_ref[target]

                @pl.when(target == z)
                def _():
                    gbown_ref[...] = sums

                @pl.when(target != z)
                def _():
                    gbsend_ref[target] = sums.astype(jnp.bfloat16)
                    gb_copy(z, target).start()

        def weight_turn(t, carry):
            out = jnp.zeros((CHUNK, cols), jnp.float32)
            for h in range(heads):
                weights = []
                folds = []
                for m in range(pieces):
                    at = piece_rows(t, m)
                    student = st_ref[h, at, :]
                    grad = student - s_ref[h, at, :] * scaling[h : h + 1, :]
                    weights.append((grad * dec_ref[h, at, :]).astype(jnp.bfloat16))
                    folds.append(fold_lanes(grad * student))
                weight = jnp.concatenate(weights, axis=0)
                w_ref[h, chunk_rows(t), :] = weight
                out = out + dot(weight, ch_ref[h], ((1,), (0,)))
                fold = jnp.concatenate(folds, axis=0)
                for k in range(blocks):
                    flipped = jnp.transpose(fold[k * 128 : (k + 1) * 128])
                    cs_ref[t * blocks + k, h : h + 1, :] = jnp.sum(
                        flipped, axis=0, keepdims=True
                    )
            gbpart_ref[pl.ds(t * per_chunk, per_chunk)] = (out * factor).reshape(
                per_chunk, 2, gb_rows, cols
            )
            gx_copy(t * per_chunk, per_chunk).start()
            return carry

        lax.fori_loop(0, steps, weight_turn, 0)
        cs_copy().start()

        for h in range(heads):
            slope_ref[ka, h : h + 1, 0:qn] = jnp.sum(
                rs_ref[h, 0], axis=0, keepdims=True
            ) - scaling[h : h + 1, :] * jnp.sum(rs_ref[h, 1], axis=0, keepdims=True)
            flat = dot(
                bt_ref[h * state : (h + 1) * state, :], w_ref[h], ((1,), (0,))
            )
            gcown_ref[:, h * state : (h + 1) * state] = jnp.transpose(flat * factor)
        gcsend_ref[...] = (
            gcown_ref[...].reshape(na, gc_rows, cols).astype(jnp.bfloat16)
        )

        cs_copy().wait_recv()
        sib_fold = jnp.sum(cssib_ref[...], axis=0)
        fold_ref[z] = jnp.sum(cs_ref[...], axis=0) + sib_fold
        mine = pl.ds(core * half, half)
        colsend_ref[...] = cs_ref[mine] + cssib_ref[mine]

        @pl.when(jnp.logical_not(diagonal))
        def _():
            col_copy(z).start()

        @pl.loop(ka, z)
        def _(target):
            fold_copy(z, target).start()

        @pl.loop(0, steps)
        def _(n):
            send_grad_b(lax.rem(n + z // per_chunk, steps))

        @pl.loop(1, na)
        def _(k):
            gc_copy(ka, lax.rem(ka + k, na)).start()

        def later_turn(slot, total):
            fold_copy(slot, z).wait_recv()
            return total + fold_ref[slot]

        later = lax.fori_loop(
            z + 1, nz, later_turn, jnp.where(core == 0, sib_fold, 0.0)
        )
        slope_ref[ka, :, qn:] = later

        @pl.when(diagonal)
        def _():
            def col_turn(slot, total):
                col_copy(slot).wait_recv()
                return total + col_ref[slot]

            above = lax.fori_loop(
                z + 1, nz, col_turn, jnp.zeros(colsend_ref.shape, jnp.float32)
            )
            everything = above + colsend_ref[...]
            for k in range(half):
                lanes = slice(k * 128, (k + 1) * 128)
                slope_ref[ka, :, lanes] = slope_ref[ka, :, lanes] - everything[k]

            @pl.when(core == 0)
            def _():
                slope_ref[ka, :, qn:] = jnp.sum(above + cssib_ref[mine], axis=0)

        @pl.loop(1, na)
        def _(k):
            slope_copy(ka, lax.rem(ka + k, na)).start()

    @pl.when(live)
    def _():
        gc_ref[...] = gcown_ref[
            pl.ds(pl.multiple_of(ka * gc_rows, gc_rows), gc_rows), :
        ]
        gb_ref[...] = gbown_ref[...]

    @pl.when(jnp.logical_not(live))
    def _():
        gc_ref[...] = jnp.zeros_like(gc_ref)
        gb_ref[...] = jnp.zeros_like(gb_ref)

    def gc_turn(slot, total):
        gc_copy(slot, slot).wait_recv()
        return total + gcrecv_ref[slot].astype(jnp.float32)

    sums = lax.fori_loop(0, jnp.minimum(ka, z + 1), gc_turn, gc_ref[...])
    gc_ref[...] = lax.fori_loop(ka + 1, z + 1, gc_turn, sums)

    def gb_turn(slot, total):
        gb_copy(slot, slot).wait_recv()
        return total + gbrecv_ref[slot].astype(jnp.float32)

    sums = lax.fori_loop(ka, z, gb_turn, gb_ref[...])
    gb_ref[...] = lax.fori_loop(jnp.maximum(ka, z + 1), nz, gb_turn, sums)

    @pl.when(live)
    def _():
        pair_copy(core).wait_send()
        to(
            gbpart_ref.at[pl.ds(0, nz), other], gbsib_ref, gx_send, gx_recv.at[0], (sibling, ka)
        ).wait_send()
        cs_copy().wait_send()

        @pl.when(jnp.logical_not(diagonal))
        def _():
            col_copy(z).wait_send()

        @pl.loop(z + 1, nz)
        def _(target):
            @pl.when(diagonal)
            def _():
                krate_copy(target).wait_send()

            @pl.when(jnp.logical_not(diagonal))
            def _():
                rfold_copy(z, target).wait_send()

        @pl.loop(ka, z)
        def _(target):
            fold_copy(z, target).wait_send()

        @pl.loop(0, z + 1)
        def _(target):
            @pl.when(target != ka)
            def _():
                stat_copy(ka, target).wait_send()

        rest = pl.ds(0, na - 1)
        to(gcsend_ref.at[rest], gcrecv_ref.at[rest], gc_send, gc_recv.at[0], (pb, ka)).wait_send()
        rest = pl.ds(0, nz - 1)
        to(gbsend_ref.at[rest], gbrecv_ref.at[rest], gb_send, gb_recv.at[0], (pb, ka)).wait_send()

    def slope_turn(slot, total):
        slope_copy(slot, slot).wait_recv()
        return total + slope_ref[slot]

    @pl.when(jnp.logical_not(live))
    def _():
        slope_ref[ka] = jnp.zeros(slope_ref.shape[1:], jnp.float32)

    both = lax.fori_loop(0, jnp.minimum(ka, z + 1), slope_turn, slope_ref[ka])
    both = lax.fori_loop(ka + 1, z + 1, slope_turn, both)
    slope = both[:, 0:qn]
    after = jnp.sum(both[:, qn:], axis=1, keepdims=True)
    scan_ref[...] = jnp.zeros_like(scan_ref)
    scan_ref[0:heads, :] = slope
    suffix = jnp.sum(slope, axis=1, keepdims=True) - lane_prefix(scan_ref[...])[0:heads, :]
    gr_ref[...] = -factor * (suffix + slope + after)

    @pl.when(live)
    def _():
        rest = pl.ds(0, na - 1)
        to(slope_ref.at[rest], slope_ref.at[rest], slope_send, slope_recv.at[0], (pb, ka)).wait_send()


def place(gc_in, gb_in, gr_in, gc_out, gb_out, gr_out, sem):
    copies = [
        pltpu.make_async_copy(src, dst, sem.at[n])
        for n, (src, dst) in enumerate(
            ((gc_in, gc_out), (gb_in, gb_out), (gr_in, gr_out))
        )
    ]
    for copy in copies:
        copy.start()
    for copy in copies:
        copy.wait()


def body(teacher_query, teacher_key, student_c, student_b, decay_rate):
    heads = decay_rate.shape[0]
    nb = lax.axis_size("pb")
    na = lax.axis_size("ka")
    qn, width = teacher_query.shape
    kn = teacher_key.shape[0]
    cols = student_c.shape[1]
    nz = nb // 2
    steps = kn // CHUNK
    f32, bf16 = jnp.float32, jnp.bfloat16
    vmem = pl.BlockSpec(memory_space=pltpu.VMEM)
    hbm = pl.BlockSpec(memory_space=pl.ANY)
    dma = pltpu.SemaphoreType.DMA
    scan_rows = -(-heads * 3 // 8) * 8
    shapes = (
        jax.ShapeDtypeStruct((qn // na, cols), f32),
        jax.ShapeDtypeStruct((kn // nb, cols), f32),
        jax.ShapeDtypeStruct((heads, qn), f32),
    )
    results = pl.pallas_call(
        functools.partial(kernel, nb, na, heads),
        out_shape=tuple(pltpu.VMEM(shape.shape, f32) for shape in shapes),
        in_specs=[hbm, hbm, hbm, hbm, hbm],
        out_specs=[vmem, vmem, vmem],
        scratch_shapes=[
            pltpu.VMEM((qn, width), bf16),
            pltpu.VMEM((kn, width), bf16),
            pltpu.VMEM((qn, cols), bf16),
            pltpu.VMEM((kn, cols), bf16),
            pltpu.VMEM((heads, qn, cols), bf16),
            pltpu.VMEM((cols, kn), bf16),
            pltpu.VMEM((heads, kn, qn), f32),
            pltpu.VMEM((heads, kn, qn), f32),
            pltpu.VMEM((heads, kn, qn), f32),
            pltpu.VMEM((heads, kn, qn), bf16),
            pltpu.VMEM((heads, kn, 128), f32),
            pltpu.VMEM((scan_rows, qn), f32),
            pltpu.VMEM((2, heads, qn), f32),
            pltpu.VMEM((2, heads, qn), f32),
            pltpu.VMEM((nz, 2, heads, 128), f32),
            pltpu.VMEM((na, 2 * heads, qn), f32),
            pltpu.VMEM((kn // 128, heads, 128), f32),
            pltpu.VMEM((kn // 128, heads, 128), f32),
            pltpu.VMEM((nz, heads, 128), f32),
            pltpu.VMEM((qn // 128, heads, 128), f32),
            pltpu.VMEM((nz, qn // 128, heads, 128), f32),
            pltpu.VMEM((na, heads, qn + 128), f32),
            pltpu.VMEM((heads, 2, 8, qn), f32),
            pltpu.VMEM((nz, 2, kn // nb, cols), f32),
            pltpu.VMEM((nz, kn // nb, cols), f32),
            pltpu.VMEM((kn // nb, cols), f32),
            pltpu.VMEM((nz, kn // nb, cols), bf16),
            pltpu.VMEM((nz, kn // nb, cols), bf16),
            pltpu.VMEM((qn, cols), f32),
            pltpu.VMEM((na, qn // na, cols), bf16),
            pltpu.VMEM((na, qn // na, cols), bf16),
            dma((5,)),
            dma,
            dma,
            dma((nz,)),
            dma,
            dma((nz,)),
            dma((na,)),
            dma((na,)),
            dma,
            dma,
            dma((nz,)),
            dma((nz,)),
            dma,
            dma((nz,)),
            dma,
            dma((na,)),
            dma,
            dma((steps,)),
            dma,
            dma((nz,)),
            dma,
            dma((na,)),
        ],
        compiler_params=pltpu.CompilerParams(
            collective_id=0, has_side_effects=True, vmem_limit_bytes=60 * 1024 * 1024
        ),
    )(teacher_query, teacher_key, student_c, student_b, decay_rate)
    return pl.pallas_call(
        place,
        out_shape=shapes,
        in_specs=[vmem, vmem, vmem],
        out_specs=[hbm, hbm, hbm],
        scratch_shapes=[dma((3,))],
    )(*results)


def solution(mesh):
    placed = (P("pb", None), P("ka", None), P("pb", None), P("ka", None), P(None, "pb"))
    return jax.shard_map(
        body,
        mesh=mesh,
        in_specs=placed,
        out_specs=(P(("pb", "ka"), None), P(("ka", "pb"), None), P(None, "pb")),
        check_vma=False,
    )
```

```python
import functools
import math

import jax
import jax.numpy as jnp
from jax import lax
from jax.experimental import pallas as pl
from jax.experimental.pallas import tpu as pltpu
from jax.sharding import PartitionSpec as P

MESH = pl.DeviceIdType.MESH
NEGATIVE = -1e30
LOG2E = 1.0 / math.log(2.0)
CHUNK = 256
PIECE = 16


def dot(a, b, dims):
    return lax.dot_general(a, b, (dims, ((), ())), preferred_element_type=jnp.float32)


def fold_rows(x):
    return jnp.sum(x.reshape(x.shape[0] // 8, 8, x.shape[1]), axis=0)


def fold_lanes(x):
    width = x.shape[1]
    out = x[:, 0:128]
    for k in range(128, width, 128):
        out = out + x[:, k : k + 128]
    return out


def lane_prefix(x):
    width = x.shape[1]
    lane = lax.broadcasted_iota(jnp.int32, x.shape, 1)
    shift = 1
    while shift < width:
        x = x + jnp.where(lane >= shift, pltpu.roll(x, shift, 1), 0.0)
        shift *= 2
    return x


def kernel(
    nb,
    na,
    heads,
    q_hbm,
    k_hbm,
    c_hbm,
    b_hbm,
    rate_hbm,
    gc_ref,
    gb_ref,
    gr_ref,
    q_ref,
    k_ref,
    c_ref,
    b_ref,
    ch_ref,
    bt_ref,
    s_ref,
    st_ref,
    dec_ref,
    w_ref,
    kcol_ref,
    scan_ref,
    rate_ref,
    krate_ref,
    rfold_ref,
    stat_ref,
    cs_ref,
    fold_ref,
    col_ref,
    slope_ref,
    rs_ref,
    gbpart_ref,
    gbsib_ref,
    gbown_ref,
    gbsend_ref,
    gbrecv_ref,
    gcown_ref,
    gcsend_ref,
    gcrecv_ref,
    in_sem,
    rate_send,
    krate_recv,
    rfold_recv,
    stat_send,
    stat_recv,
    fold_send,
    fold_recv,
    col_send,
    col_recv,
    slope_send,
    slope_recv,
    gx_send,
    gx_recv,
    gb_send,
    gb_recv,
    gc_send,
    gc_recv,
):
    pb = lax.axis_index("pb")
    ka = lax.axis_index("ka")
    qn, width = q_ref.shape
    kn = k_ref.shape[0]
    dh = width // heads
    cols = c_ref.shape[1]
    state = cols // heads
    nz = nb // 2
    z = pb // 2
    core = lax.rem(pb, 2)
    other = 1 - core
    sibling = 2 * z + other
    steps = kn // CHUNK
    half = qn // 128
    pieces = CHUNK // PIECE
    blocks = CHUNK // 128
    gb_rows = kn // nb
    gc_rows = qn // na
    per_chunk = CHUNK // (2 * gb_rows)
    factor = 2.0 * qn * nb
    first = 2 * ka
    live = z >= ka
    diagonal = z == ka

    loads = [
        pltpu.make_async_copy(src, dst, in_sem.at[n])
        for n, (src, dst) in enumerate(
            (
                (q_hbm, q_ref),
                (k_hbm, k_ref),
                (rate_hbm, rate_ref),
                (c_hbm, c_ref),
                (b_hbm, b_ref),
            )
        )
    ]
    for load in loads:
        load.start()

    barrier = pltpu.get_barrier_semaphore()

    @pl.loop(1, na)
    def _(k):
        pl.semaphore_signal(
            barrier, inc=1, device_id=(pb, lax.rem(ka + k, na)), device_id_type=MESH
        )

    @pl.loop(1, nb)
    def _(k):
        pl.semaphore_signal(
            barrier, inc=1, device_id=(lax.rem(pb + k, nb), ka), device_id_type=MESH
        )

    def to(src, dst, send, recv, device):
        return pltpu.make_async_remote_copy(
            src_ref=src,
            dst_ref=dst,
            send_sem=send,
            recv_sem=recv,
            device_id=device,
            device_id_type=MESH,
        )

    def up(target):
        return (2 * target + core, ka)

    def krate_copy(slot, target):
        return to(
            rate_ref,
            krate_ref.at[slot],
            rate_send.at[target],
            krate_recv.at[slot],
            (target, ka),
        )

    def rfold_copy(slot, target):
        return to(
            rfold_ref.at[slot],
            rfold_ref.at[slot],
            rate_send.at[target],
            rfold_recv.at[slot],
            (target, ka),
        )

    def stat_copy(slot, target):
        return to(
            stat_ref.at[slot],
            stat_ref.at[slot],
            stat_send.at[target],
            stat_recv.at[slot],
            (pb, target),
        )

    def fold_copy(slot, target):
        return to(
            fold_ref.at[slot],
            fold_ref.at[slot],
            fold_send.at[target],
            fold_recv.at[slot],
            (target, ka),
        )

    def col_copy(part, slot):
        return to(
            cs_ref.at[pl.ds(part * half, half)],
            col_ref.at[slot],
            col_send.at[part],
            col_recv.at[slot],
            (first + part, ka),
        )

    def slope_copy(slot, target):
        return to(
            slope_ref.at[slot],
            slope_ref.at[slot],
            slope_send,
            slope_recv.at[slot],
            (pb, target),
        )

    def gx_copy(start, count):
        return to(
            gbpart_ref.at[pl.ds(start, count), other],
            gbsib_ref.at[pl.ds(start, count)],
            gx_send,
            gx_recv.at[start // per_chunk],
            (sibling, ka),
        )

    def gb_copy(slot, target):
        return to(
            gbsend_ref.at[target],
            gbrecv_ref.at[slot],
            gb_send,
            gb_recv.at[slot],
            up(target),
        )

    def gc_copy(slot, target):
        return to(
            gcsend_ref.at[target],
            gcrecv_ref.at[slot],
            gc_send,
            gc_recv.at[slot],
            (pb, target),
        )

    offset = pb * qn - ka * kn

    def mask_of(t, piece):
        rows = lax.broadcasted_iota(jnp.int32, (PIECE, qn), 0)
        lanes = lax.broadcasted_iota(jnp.int32, (PIECE, qn), 1)
        return lanes - rows >= t * CHUNK + piece * PIECE - offset

    def piece_rows(t, piece):
        return pl.ds(pl.multiple_of(t * CHUNK + piece * PIECE, PIECE), PIECE)

    def chunk_rows(t):
        return pl.ds(pl.multiple_of(t * CHUNK, CHUNK), CHUNK)

    scale2 = LOG2E / math.sqrt(dh)

    def head_stats(h, masked):
        lanes = slice(h * dh, (h + 1) * dh)

        def score_turn(t, peak):
            s = dot(k_ref[chunk_rows(t), lanes], q_ref[:, lanes], ((1,), (1,)))
            for n in range(pieces):
                part = s[n * PIECE : (n + 1) * PIECE] * scale2
                if masked:
                    part = jnp.where(mask_of(t, n), part, NEGATIVE)
                s_ref[h, piece_rows(t, n), :] = part
                for k in range(0, PIECE, 8):
                    peak = jnp.maximum(peak, part[k : k + 8])
            return peak

        peak = lax.fori_loop(
            0, steps, score_turn, jnp.full((8, qn), NEGATIVE, jnp.float32)
        )
        peak = jnp.max(peak, axis=0, keepdims=True)

        def expo_turn(t, total):
            for n in range(pieces):
                e = jnp.exp2(s_ref[h, piece_rows(t, n), :] - peak)
                s_ref[h, piece_rows(t, n), :] = e
                for k in range(0, PIECE, 8):
                    total = total + e[k : k + 8]
            return total

        total = lax.fori_loop(0, steps, expo_turn, jnp.zeros((8, qn), jnp.float32))
        stat_ref[ka, h : h + 1, :] = peak
        stat_ref[ka, heads + h : heads + h + 1, :] = jnp.sum(
            total, axis=0, keepdims=True
        )

    def stats(first, last):
        @pl.when(diagonal)
        def _():
            for h in range(first, last):
                head_stats(h, True)

        @pl.when(z > ka)
        def _():
            for h in range(first, last):
                head_stats(h, False)

    @pl.when(live)
    def _():
        stat_init = jnp.concatenate(
            [
                jnp.full((heads, qn), NEGATIVE, jnp.float32),
                jnp.zeros((heads, qn), jnp.float32),
            ],
            axis=0,
        )

        @pl.loop(z + 1, na)
        def _(slot):
            stat_ref[slot] = stat_init

    loads[0].wait()
    loads[1].wait()

    stats(0, heads)

    for load in loads[2:]:
        load.wait()
    pl.semaphore_wait(barrier, na + nb - 2)

    @pl.when(live)
    def _():
        rfold_ref[pb] = fold_lanes(rate_ref[...])

        @pl.loop(pb + 1, nb)
        def _(target):
            @pl.when(diagonal)
            def _():
                krate_copy(core, target).start()

            @pl.when(jnp.logical_not(diagonal))
            def _():
                rfold_copy(pb, target).start()

        @pl.loop(1, na)
        def _(k):
            target = lax.rem(ka + k, na)

            @pl.when(target <= z)
            def _():
                stat_copy(ka, target).start()

        head_of = lax.broadcasted_iota(jnp.int32, (qn, cols), 1) // state
        c_all = c_ref[...]
        for h in range(heads):
            ch_ref[h] = jnp.where(head_of == h, c_all, jnp.zeros_like(c_all))
        bt_ref[...] = jnp.transpose(b_ref[...])

        @pl.when(diagonal)
        def _():
            krate_ref[core] = rate_ref[...]

            @pl.when(core == 0)
            def _():
                krate_ref[1] = jnp.zeros_like(rate_ref)

        @pl.when(pb > first)
        def _():
            krate_copy(0, pb).wait_recv()

        @pl.when(z > ka)
        def _():
            krate_copy(1, pb).wait_recv()

        scan_ref[...] = jnp.zeros_like(scan_ref)
        scan_ref[0:heads, :] = rate_ref[...]
        for part in range(2):
            low = heads * (1 + part)
            scan_ref[low : low + heads, :] = krate_ref[part]

        rates = scan_ref[...]
        scan_ref[...] = lane_prefix(rates)
        ends = jnp.sum(rates, axis=1, keepdims=True)
        for h in range(heads):
            shift = jnp.zeros((1, 1), jnp.float32)
            for part in range(2):
                row = heads * (1 + part) + h
                prefix = (scan_ref[row : row + 1, :] + shift) * LOG2E
                kcol_ref[h, part * qn : (part + 1) * qn, :] = jnp.transpose(
                    jnp.broadcast_to(prefix, (128, qn))
                )
                shift = shift + ends[row : row + 1, :]

        def between_turn(slot, total):
            rfold_copy(slot, pb).wait_recv()
            return total + rfold_ref[slot]

        between = lax.fori_loop(
            first + 2, pb, between_turn, jnp.zeros((heads, 128), jnp.float32)
        )
        before = (
            jnp.sum(between, axis=1, keepdims=True)
            + jnp.where(pb > first, ends[heads : 2 * heads], 0.0)
            + jnp.where(z > ka, ends[2 * heads : 3 * heads], 0.0)
        )
        arow = (scan_ref[0:heads, :] + before) * LOG2E

        def student_pass(masked):
            def student_turn(t, sums):
                b_rows = b_ref[chunk_rows(t), :]
                inners = [dot(b_rows, ch_ref[h], ((1,), (1,))) for h in range(heads)]
                new_sums = []
                for h in range(heads):
                    squares, mixed = sums[h]
                    for m in range(pieces):
                        at = piece_rows(t, m)
                        column = kcol_ref[h, at, :]
                        gap = (
                            jnp.concatenate([column] * (qn // 128), axis=1)
                            - arow[h : h + 1, :]
                        )
                        if masked:
                            gap = jnp.where(mask_of(t, m), gap, NEGATIVE)
                        decay = jnp.exp2(gap)
                        student = inners[h][m * PIECE : (m + 1) * PIECE] * decay
                        dec_ref[h, at, :] = decay
                        st_ref[h, at, :] = student
                        square = student * student
                        mix = student * s_ref[h, at, :]
                        for k in range(0, PIECE, 8):
                            squares = squares + square[k : k + 8]
                            mixed = mixed + mix[k : k + 8]
                    new_sums.append((squares, mixed))
                return tuple(new_sums)

            zero = jnp.zeros((8, qn), jnp.float32)
            sums = lax.fori_loop(
                0, steps, student_turn, tuple((zero, zero) for _ in range(heads))
            )
            for h in range(heads):
                rs_ref[h, 0] = sums[h][0]
                rs_ref[h, 1] = sums[h][1]

        @pl.when(diagonal)
        def _():
            student_pass(True)

        @pl.when(z > ka)
        def _():
            student_pass(False)

        @pl.loop(0, z + 1)
        def _(slot):
            @pl.when(slot != ka)
            def _():
                stat_copy(slot, slot).wait_recv()

        peaks = stat_ref[:, 0:heads, :]
        totals = stat_ref[:, heads : 2 * heads, :]
        peak = jnp.max(peaks, axis=0)
        total = jnp.sum(totals * jnp.exp2(peaks - peak[None]), axis=0)
        own_peak = stat_ref[ka, 0:heads, :]
        scaling = jnp.exp2(own_peak - peak) / total

        def send_grad_b(t):
            gx_copy(t * per_chunk, per_chunk).wait_recv()

            @pl.loop(0, per_chunk)
            def _(k):
                target = t * per_chunk + k
                sums = gbpart_ref[target, core] + gbsib_ref[target]

                @pl.when(target == z)
                def _():
                    gbown_ref[...] = sums

                @pl.when(target != z)
                def _():
                    gbsend_ref[target] = sums.astype(jnp.bfloat16)
                    gb_copy(z, target).start()

        def column_turn(t, carry):
            for h in range(heads):
                folds = []
                for m in range(pieces):
                    at = piece_rows(t, m)
                    student = st_ref[h, at, :]
                    grad = student - s_ref[h, at, :] * scaling[h : h + 1, :]
                    folds.append(fold_lanes(grad * student))
                fold = jnp.concatenate(folds, axis=0)
                for k in range(blocks):
                    flipped = jnp.transpose(fold[k * 128 : (k + 1) * 128])
                    cs_ref[t * blocks + k, h : h + 1, :] = jnp.sum(
                        flipped, axis=0, keepdims=True
                    )
            return carry

        lax.fori_loop(0, steps, column_turn, 0)
        fold_ref[pb] = jnp.sum(cs_ref[...], axis=0)

        for part in range(2):

            @pl.when(pb != first + part)
            def _(part=part):
                col_copy(part, pb).start()

        @pl.loop(first, pb)
        def _(target):
            fold_copy(pb, target).start()

        def weight_turn(t, carry):
            out = jnp.zeros((CHUNK, cols), jnp.float32)
            for h in range(heads):
                weights = []
                for m in range(pieces):
                    at = piece_rows(t, m)
                    student = st_ref[h, at, :]
                    grad = student - s_ref[h, at, :] * scaling[h : h + 1, :]
                    weights.append((grad * dec_ref[h, at, :]).astype(jnp.bfloat16))
                weight = jnp.concatenate(weights, axis=0)
                w_ref[h, chunk_rows(t), :] = weight
                out = out + dot(weight, ch_ref[h], ((1,), (0,)))
            gbpart_ref[pl.ds(t * per_chunk, per_chunk)] = (out * factor).reshape(
                per_chunk, 2, gb_rows, cols
            )
            gx_copy(t * per_chunk, per_chunk).start()
            return carry

        lax.fori_loop(0, steps, weight_turn, 0)

        for h in range(heads):
            slope_ref[ka, h : h + 1, 0:qn] = jnp.sum(
                rs_ref[h, 0], axis=0, keepdims=True
            ) - scaling[h : h + 1, :] * jnp.sum(rs_ref[h, 1], axis=0, keepdims=True)
            flat = dot(
                bt_ref[h * state : (h + 1) * state, :], w_ref[h], ((1,), (0,))
            )
            gcown_ref[:, h * state : (h + 1) * state] = jnp.transpose(flat * factor)
        gcsend_ref[...] = (
            gcown_ref[...].reshape(na, gc_rows, cols).astype(jnp.bfloat16)
        )

        @pl.loop(0, steps)
        def _(n):
            send_grad_b(lax.rem(n + z // per_chunk, steps))

        @pl.loop(1, na)
        def _(k):
            gc_copy(ka, lax.rem(ka + k, na)).start()

        def later_turn(slot, total):
            fold_copy(slot, pb).wait_recv()
            return total + fold_ref[slot]

        slope_ref[ka, :, qn:] = lax.fori_loop(
            pb + 1, nb, later_turn, jnp.zeros((heads, 128), jnp.float32)
        )

        @pl.when(diagonal)
        def _():
            def col_turn(slot, total):
                col_copy(0, slot).wait_recv()
                return total + col_ref[slot]

            others = lax.fori_loop(
                first, pb, col_turn, jnp.zeros(col_ref.shape[1:], jnp.float32)
            )
            others = lax.fori_loop(pb + 1, nb, col_turn, others)
            everything = others + cs_ref[pl.ds(core * half, half)]
            for k in range(half):
                lanes = slice(k * 128, (k + 1) * 128)
                slope_ref[ka, :, lanes] = slope_ref[ka, :, lanes] - everything[k]

            @pl.when(core == 0)
            def _():
                slope_ref[ka, :, qn:] = jnp.sum(others, axis=0)

        @pl.loop(1, na)
        def _(k):
            slope_copy(ka, lax.rem(ka + k, na)).start()

    @pl.when(live)
    def _():
        gc_ref[...] = gcown_ref[
            pl.ds(pl.multiple_of(ka * gc_rows, gc_rows), gc_rows), :
        ]
        gb_ref[...] = gbown_ref[...]

    @pl.when(jnp.logical_not(live))
    def _():
        gc_ref[...] = jnp.zeros_like(gc_ref)
        gb_ref[...] = jnp.zeros_like(gb_ref)

    def gc_turn(slot, total):
        gc_copy(slot, slot).wait_recv()
        return total + gcrecv_ref[slot].astype(jnp.float32)

    sums = lax.fori_loop(0, jnp.minimum(ka, z + 1), gc_turn, gc_ref[...])
    gc_ref[...] = lax.fori_loop(ka + 1, z + 1, gc_turn, sums)

    def gb_turn(slot, total):
        gb_copy(slot, slot).wait_recv()
        return total + gbrecv_ref[slot].astype(jnp.float32)

    sums = lax.fori_loop(ka, z, gb_turn, gb_ref[...])
    gb_ref[...] = lax.fori_loop(jnp.maximum(ka, z + 1), nz, gb_turn, sums)

    @pl.when(live)
    def _():
        to(
            gbpart_ref.at[pl.ds(0, nz), other], gbsib_ref, gx_send, gx_recv.at[0], (sibling, ka)
        ).wait_send()

        for part in range(2):

            @pl.when(pb != first + part)
            def _(part=part):
                col_copy(part, pb).wait_send()

        @pl.loop(pb + 1, nb)
        def _(target):
            @pl.when(diagonal)
            def _():
                krate_copy(core, target).wait_send()

            @pl.when(jnp.logical_not(diagonal))
            def _():
                rfold_copy(pb, target).wait_send()

        @pl.loop(first, pb)
        def _(target):
            fold_copy(pb, target).wait_send()

        @pl.loop(0, z + 1)
        def _(target):
            @pl.when(target != ka)
            def _():
                stat_copy(ka, target).wait_send()

        rest = pl.ds(0, na - 1)
        to(gcsend_ref.at[rest], gcrecv_ref.at[rest], gc_send, gc_recv.at[0], (pb, ka)).wait_send()
        rest = pl.ds(0, nz - 1)
        to(gbsend_ref.at[rest], gbrecv_ref.at[rest], gb_send, gb_recv.at[0], (pb, ka)).wait_send()

    def slope_turn(slot, total):
        slope_copy(slot, slot).wait_recv()
        return total + slope_ref[slot]

    @pl.when(jnp.logical_not(live))
    def _():
        slope_ref[ka] = jnp.zeros(slope_ref.shape[1:], jnp.float32)

    both = lax.fori_loop(0, jnp.minimum(ka, z + 1), slope_turn, slope_ref[ka])
    both = lax.fori_loop(ka + 1, z + 1, slope_turn, both)
    slope = both[:, 0:qn]
    after = jnp.sum(both[:, qn:], axis=1, keepdims=True)
    scan_ref[...] = jnp.zeros_like(scan_ref)
    scan_ref[0:heads, :] = slope
    suffix = jnp.sum(slope, axis=1, keepdims=True) - lane_prefix(scan_ref[...])[0:heads, :]
    gr_ref[...] = -factor * (suffix + slope + after)

    @pl.when(live)
    def _():
        rest = pl.ds(0, na - 1)
        to(slope_ref.at[rest], slope_ref.at[rest], slope_send, slope_recv.at[0], (pb, ka)).wait_send()


def place(gc_in, gb_in, gr_in, gc_out, gb_out, gr_out, gc, gb, gr, sem):
    triples = ((gc_in, gc, gc_out), (gb_in, gb, gb_out), (gr_in, gr, gr_out))
    loads = [
        pltpu.make_async_copy(src, held, sem.at[n])
        for n, (src, held, _) in enumerate(triples)
    ]
    stores = [
        pltpu.make_async_copy(held, dst, sem.at[n])
        for n, (_, held, dst) in enumerate(triples)
    ]
    for load in loads:
        load.start()
    for load, store in zip(loads, stores):
        load.wait()
        store.start()
    for store in stores:
        store.wait()


def body(teacher_query, teacher_key, student_c, student_b, decay_rate):
    heads = decay_rate.shape[0]
    nb = lax.axis_size("pb")
    na = lax.axis_size("ka")
    qn, width = teacher_query.shape
    kn = teacher_key.shape[0]
    cols = student_c.shape[1]
    nz = nb // 2
    steps = kn // CHUNK
    f32, bf16 = jnp.float32, jnp.bfloat16
    vmem = pl.BlockSpec(memory_space=pltpu.VMEM)
    hbm = pl.BlockSpec(memory_space=pl.ANY)
    dma = pltpu.SemaphoreType.DMA
    scan_rows = -(-heads * 3 // 8) * 8
    shapes = (
        jax.ShapeDtypeStruct((qn // na, cols), f32),
        jax.ShapeDtypeStruct((kn // nb, cols), f32),
        jax.ShapeDtypeStruct((heads, qn), f32),
    )
    results = pl.pallas_call(
        functools.partial(kernel, nb, na, heads),
        out_shape=shapes,
        in_specs=[hbm, hbm, hbm, hbm, hbm],
        out_specs=[vmem, vmem, vmem],
        scratch_shapes=[
            pltpu.VMEM((qn, width), bf16),
            pltpu.VMEM((kn, width), bf16),
            pltpu.VMEM((qn, cols), bf16),
            pltpu.VMEM((kn, cols), bf16),
            pltpu.VMEM((heads, qn, cols), bf16),
            pltpu.VMEM((cols, kn), bf16),
            pltpu.VMEM((heads, kn, qn), f32),
            pltpu.VMEM((heads, kn, qn), f32),
            pltpu.VMEM((heads, kn, qn), f32),
            pltpu.VMEM((heads, kn, qn), bf16),
            pltpu.VMEM((heads, kn, 128), f32),
            pltpu.VMEM((scan_rows, qn), f32),
            pltpu.VMEM((heads, qn), f32),
            pltpu.VMEM((2, heads, qn), f32),
            pltpu.VMEM((nb, heads, 128), f32),
            pltpu.VMEM((na, 2 * heads, qn), f32),
            pltpu.VMEM((kn // 128, heads, 128), f32),
            pltpu.VMEM((nb, heads, 128), f32),
            pltpu.VMEM((nb, qn // 128, heads, 128), f32),
            pltpu.VMEM((na, heads, qn + 128), f32),
            pltpu.VMEM((heads, 2, 8, qn), f32),
            pltpu.VMEM((nz, 2, kn // nb, cols), f32),
            pltpu.VMEM((nz, kn // nb, cols), f32),
            pltpu.VMEM((kn // nb, cols), f32),
            pltpu.VMEM((nz, kn // nb, cols), bf16),
            pltpu.VMEM((nz, kn // nb, cols), bf16),
            pltpu.VMEM((qn, cols), f32),
            pltpu.VMEM((na, qn // na, cols), bf16),
            pltpu.VMEM((na, qn // na, cols), bf16),
            dma((5,)),
            dma((nb,)),
            dma((2,)),
            dma((nb,)),
            dma((na,)),
            dma((na,)),
            dma((nb,)),
            dma((nb,)),
            dma((2,)),
            dma((nb,)),
            dma,
            dma((na,)),
            dma,
            dma((steps,)),
            dma,
            dma((nz,)),
            dma,
            dma((na,)),
        ],
        compiler_params=pltpu.CompilerParams(
            collective_id=0, has_side_effects=True, vmem_limit_bytes=62 * 1024 * 1024
        ),
    )(teacher_query, teacher_key, student_c, student_b, decay_rate)
    return pl.pallas_call(
        place,
        out_shape=shapes,
        in_specs=[hbm, hbm, hbm],
        out_specs=[hbm, hbm, hbm],
        scratch_shapes=[pltpu.VMEM(shape.shape, f32) for shape in shapes] + [dma((3,))],
        compiler_params=pltpu.CompilerParams(vmem_limit_bytes=62 * 1024 * 1024),
    )(*results)


def solution(mesh):
    placed = (P("pb", None), P("ka", None), P("pb", None), P("ka", None), P(None, "pb"))
    return jax.shard_map(
        body,
        mesh=mesh,
        in_specs=placed,
        out_specs=(P(("pb", "ka"), None), P(("ka", "pb"), None), P(None, "pb")),
        check_vma=False,
    )
```

```python
import functools
import math

import jax
import jax.numpy as jnp
from jax import lax
from jax.experimental import pallas as pl
from jax.experimental.pallas import tpu as pltpu
from jax.sharding import PartitionSpec as P

MESH = pl.DeviceIdType.MESH
NEGATIVE = -1e30
LOG2E = 1.0 / math.log(2.0)
CHUNK = 256
PIECE = 16


def dot(a, b, dims):
    return lax.dot_general(a, b, (dims, ((), ())), preferred_element_type=jnp.float32)


def fold_rows(x):
    return jnp.sum(x.reshape(x.shape[0] // 8, 8, x.shape[1]), axis=0)


def fold_lanes(x):
    width = x.shape[1]
    out = x[:, 0:128]
    for k in range(128, width, 128):
        out = out + x[:, k : k + 128]
    return out


def lane_prefix(x):
    width = x.shape[1]
    lane = lax.broadcasted_iota(jnp.int32, x.shape, 1)
    shift = 1
    while shift < width:
        x = x + jnp.where(lane >= shift, pltpu.roll(x, shift, 1), 0.0)
        shift *= 2
    return x


def kernel(
    nb,
    na,
    heads,
    q_hbm,
    k_hbm,
    c_hbm,
    b_hbm,
    rate_hbm,
    gc_ref,
    gb_ref,
    gr_ref,
    q_ref,
    k_ref,
    c_ref,
    b_ref,
    ch_ref,
    bt_ref,
    s_ref,
    st_ref,
    dec_ref,
    w_ref,
    kcol_ref,
    scan_ref,
    rate_ref,
    krate_ref,
    rfold_ref,
    stat_ref,
    peak_ref,
    cs_ref,
    fold_ref,
    col_ref,
    slope_ref,
    rs_ref,
    gbpart_ref,
    gbsib_ref,
    gbown_ref,
    gbsend_ref,
    gbrecv_ref,
    gcown_ref,
    gcsend_ref,
    gcrecv_ref,
    in_sem,
    rate_send,
    krate_recv,
    rfold_recv,
    stat_send,
    stat_recv,
    fold_send,
    fold_recv,
    col_send,
    col_recv,
    slope_send,
    slope_recv,
    gx_send,
    gx_recv,
    gb_send,
    gb_recv,
    gc_send,
    gc_recv,
):
    pb = lax.axis_index("pb")
    ka = lax.axis_index("ka")
    qn, width = q_ref.shape
    kn = k_ref.shape[0]
    dh = width // heads
    cols = c_ref.shape[1]
    state = cols // heads
    nz = nb // 2
    z = pb // 2
    core = lax.rem(pb, 2)
    other = 1 - core
    sibling = 2 * z + other
    steps = kn // CHUNK
    half = qn // 128
    pieces = CHUNK // PIECE
    blocks = CHUNK // 128
    gb_rows = kn // nb
    gc_rows = qn // na
    per_chunk = CHUNK // (2 * gb_rows)
    factor = 2.0 * qn * nb
    first = 2 * ka
    live = z >= ka
    diagonal = z == ka

    loads = [
        pltpu.make_async_copy(src, dst, in_sem.at[n])
        for n, (src, dst) in enumerate(
            (
                (q_hbm, q_ref),
                (k_hbm, k_ref),
                (rate_hbm, rate_ref),
                (c_hbm, c_ref),
                (b_hbm, b_ref),
            )
        )
    ]
    for load in loads:
        load.start()

    barrier = pltpu.get_barrier_semaphore()

    @pl.loop(1, na)
    def _(k):
        pl.semaphore_signal(
            barrier, inc=1, device_id=(pb, lax.rem(ka + k, na)), device_id_type=MESH
        )

    @pl.loop(1, nb)
    def _(k):
        pl.semaphore_signal(
            barrier, inc=1, device_id=(lax.rem(pb + k, nb), ka), device_id_type=MESH
        )

    def to(src, dst, send, recv, device):
        return pltpu.make_async_remote_copy(
            src_ref=src,
            dst_ref=dst,
            send_sem=send,
            recv_sem=recv,
            device_id=device,
            device_id_type=MESH,
        )

    def up(target):
        return (2 * target + core, ka)

    def krate_copy(slot, target):
        return to(
            rate_ref,
            krate_ref.at[slot],
            rate_send.at[target],
            krate_recv.at[slot],
            (target, ka),
        )

    def rfold_copy(slot, target):
        return to(
            rfold_ref.at[slot],
            rfold_ref.at[slot],
            rate_send.at[target],
            rfold_recv.at[slot],
            (target, ka),
        )

    def stat_copy(slot, target):
        return to(
            stat_ref.at[slot],
            stat_ref.at[slot],
            stat_send.at[target],
            stat_recv.at[slot],
            (pb, target),
        )

    def fold_copy(slot, target):
        return to(
            fold_ref.at[slot],
            fold_ref.at[slot],
            fold_send.at[target],
            fold_recv.at[slot],
            (target, ka),
        )

    def col_copy(part, slot):
        return to(
            cs_ref.at[pl.ds(part * half, half)],
            col_ref.at[slot],
            col_send.at[part],
            col_recv.at[slot],
            (first + part, ka),
        )

    def slope_copy(slot, target):
        return to(
            slope_ref.at[slot],
            slope_ref.at[slot],
            slope_send,
            slope_recv.at[slot],
            (pb, target),
        )

    def gx_copy(start, count):
        return to(
            gbpart_ref.at[pl.ds(start, count), other],
            gbsib_ref.at[pl.ds(start, count)],
            gx_send,
            gx_recv.at[start // per_chunk],
            (sibling, ka),
        )

    def gb_copy(slot, target):
        return to(
            gbsend_ref.at[target],
            gbrecv_ref.at[slot],
            gb_send,
            gb_recv.at[slot],
            up(target),
        )

    def gc_copy(slot, target):
        return to(
            gcsend_ref.at[target],
            gcrecv_ref.at[slot],
            gc_send,
            gc_recv.at[slot],
            (pb, target),
        )

    offset = pb * qn - ka * kn

    def mask_of(t, piece):
        rows = lax.broadcasted_iota(jnp.int32, (PIECE, qn), 0)
        lanes = lax.broadcasted_iota(jnp.int32, (PIECE, qn), 1)
        return lanes - rows >= t * CHUNK + piece * PIECE - offset

    def piece_rows(t, piece):
        return pl.ds(pl.multiple_of(t * CHUNK + piece * PIECE, PIECE), PIECE)

    def chunk_rows(t):
        return pl.ds(pl.multiple_of(t * CHUNK, CHUNK), CHUNK)

    scale2 = LOG2E / math.sqrt(dh)

    def head_stats(h, masked):
        lanes = slice(h * dh, (h + 1) * dh)

        def score_turn(t, peak):
            s = dot(k_ref[chunk_rows(t), lanes], q_ref[:, lanes], ((1,), (1,)))
            for n in range(pieces):
                part = s[n * PIECE : (n + 1) * PIECE] * scale2
                if masked:
                    part = jnp.where(mask_of(t, n), part, NEGATIVE)
                s_ref[h, piece_rows(t, n), :] = part
                for k in range(0, PIECE, 8):
                    peak = jnp.maximum(peak, part[k : k + 8])
            return peak

        peak = lax.fori_loop(
            0, steps, score_turn, jnp.full((8, qn), NEGATIVE, jnp.float32)
        )
        peak = jnp.max(peak, axis=0, keepdims=True)

        def expo_turn(t, total):
            for n in range(pieces):
                e = jnp.exp2(s_ref[h, piece_rows(t, n), :] - peak)
                s_ref[h, piece_rows(t, n), :] = e
                for k in range(0, PIECE, 8):
                    total = total + e[k : k + 8]
            return total

        total = lax.fori_loop(0, steps, expo_turn, jnp.zeros((8, qn), jnp.float32))
        peak_ref[h : h + 1, :] = peak
        stat_ref[ka, h : h + 1, :] = peak + jnp.log2(
            jnp.sum(total, axis=0, keepdims=True)
        )

    def stats(first, last):
        @pl.when(diagonal)
        def _():
            for h in range(first, last):
                head_stats(h, True)

        @pl.when(z > ka)
        def _():
            for h in range(first, last):
                head_stats(h, False)

    @pl.when(live)
    def _():
        stat_init = jnp.full((heads, qn), NEGATIVE, jnp.float32)

        @pl.loop(z + 1, na)
        def _(slot):
            stat_ref[slot] = stat_init

    loads[0].wait()
    loads[1].wait()

    stats(0, heads)

    for load in loads[2:]:
        load.wait()
    pl.semaphore_wait(barrier, na + nb - 2)

    @pl.when(live)
    def _():
        rfold_ref[pb] = fold_lanes(rate_ref[...])

        @pl.loop(pb + 1, nb)
        def _(target):
            @pl.when(diagonal)
            def _():
                krate_copy(core, target).start()

            @pl.when(jnp.logical_not(diagonal))
            def _():
                rfold_copy(pb, target).start()

        @pl.loop(1, na)
        def _(k):
            target = lax.rem(ka + k, na)

            @pl.when(target <= z)
            def _():
                stat_copy(ka, target).start()

        head_of = lax.broadcasted_iota(jnp.int32, (qn, cols), 1) // state
        c_all = c_ref[...]
        for h in range(heads):
            ch_ref[h] = jnp.where(head_of == h, c_all, jnp.zeros_like(c_all))
        bt_ref[...] = jnp.transpose(b_ref[...])

        @pl.when(diagonal)
        def _():
            krate_ref[core] = rate_ref[...]

            @pl.when(core == 0)
            def _():
                krate_ref[1] = jnp.zeros_like(rate_ref)

        @pl.when(pb > first)
        def _():
            krate_copy(0, pb).wait_recv()

        @pl.when(z > ka)
        def _():
            krate_copy(1, pb).wait_recv()

        scan_ref[...] = jnp.zeros_like(scan_ref)
        scan_ref[0:heads, :] = rate_ref[...]
        for part in range(2):
            low = heads * (1 + part)
            scan_ref[low : low + heads, :] = krate_ref[part]

        rates = scan_ref[...]
        scan_ref[...] = lane_prefix(rates)
        ends = jnp.sum(rates, axis=1, keepdims=True)
        for h in range(heads):
            shift = jnp.zeros((1, 1), jnp.float32)
            for part in range(2):
                row = heads * (1 + part) + h
                prefix = (scan_ref[row : row + 1, :] + shift) * LOG2E
                kcol_ref[h, part * qn : (part + 1) * qn, :] = jnp.transpose(
                    jnp.broadcast_to(prefix, (128, qn))
                )
                shift = shift + ends[row : row + 1, :]

        def between_turn(slot, total):
            rfold_copy(slot, pb).wait_recv()
            return total + rfold_ref[slot]

        between = lax.fori_loop(
            first + 2, pb, between_turn, jnp.zeros((heads, 128), jnp.float32)
        )
        before = (
            jnp.sum(between, axis=1, keepdims=True)
            + jnp.where(pb > first, ends[heads : 2 * heads], 0.0)
            + jnp.where(z > ka, ends[2 * heads : 3 * heads], 0.0)
        )
        arow = (scan_ref[0:heads, :] + before) * LOG2E

        def student_pass(masked):
            def student_turn(t, sums):
                b_rows = b_ref[chunk_rows(t), :]
                inners = [dot(b_rows, ch_ref[h], ((1,), (1,))) for h in range(heads)]
                new_sums = []
                for h in range(heads):
                    squares, mixed = sums[h]
                    for m in range(pieces):
                        at = piece_rows(t, m)
                        column = kcol_ref[h, at, :]
                        gap = (
                            jnp.concatenate([column] * (qn // 128), axis=1)
                            - arow[h : h + 1, :]
                        )
                        if masked:
                            gap = jnp.where(mask_of(t, m), gap, NEGATIVE)
                        decay = jnp.exp2(gap)
                        student = inners[h][m * PIECE : (m + 1) * PIECE] * decay
                        dec_ref[h, at, :] = decay
                        st_ref[h, at, :] = student
                        square = student * student
                        mix = student * s_ref[h, at, :]
                        for k in range(0, PIECE, 8):
                            squares = squares + square[k : k + 8]
                            mixed = mixed + mix[k : k + 8]
                    new_sums.append((squares, mixed))
                return tuple(new_sums)

            zero = jnp.zeros((8, qn), jnp.float32)
            sums = lax.fori_loop(
                0, steps, student_turn, tuple((zero, zero) for _ in range(heads))
            )
            for h in range(heads):
                rs_ref[h, 0] = sums[h][0]
                rs_ref[h, 1] = sums[h][1]

        @pl.when(diagonal)
        def _():
            student_pass(True)

        @pl.when(z > ka)
        def _():
            student_pass(False)

        @pl.loop(0, z + 1)
        def _(slot):
            @pl.when(slot != ka)
            def _():
                stat_copy(slot, slot).wait_recv()

        parts = stat_ref[...]
        peak = jnp.max(parts, axis=0)
        total = jnp.sum(jnp.exp2(parts - peak[None]), axis=0)
        scaling = jnp.exp2(peak_ref[...] - (peak + jnp.log2(total)))

        def send_grad_b(t):
            gx_copy(t * per_chunk, per_chunk).wait_recv()

            @pl.loop(0, per_chunk)
            def _(k):
                target = t * per_chunk + k
                sums = gbpart_ref[target, core] + gbsib_ref[target]

                @pl.when(target == z)
                def _():
                    gbown_ref[...] = sums

                @pl.when(target != z)
                def _():
                    gbsend_ref[target] = sums.astype(jnp.bfloat16)
                    gb_copy(z, target).start()

        def column_turn(t, carry):
            for h in range(heads):
                folds = []
                for m in range(pieces):
                    at = piece_rows(t, m)
                    student = st_ref[h, at, :]
                    grad = student - s_ref[h, at, :] * scaling[h : h + 1, :]
                    folds.append(fold_lanes(grad * student))
                fold = jnp.concatenate(folds, axis=0)
                for k in range(blocks):
                    flipped = jnp.transpose(fold[k * 128 : (k + 1) * 128])
                    cs_ref[t * blocks + k, h : h + 1, :] = jnp.sum(
                        flipped, axis=0, keepdims=True
                    )
            return carry

        lax.fori_loop(0, steps, column_turn, 0)
        fold_ref[pb] = jnp.sum(cs_ref[...], axis=0)

        for part in range(2):

            @pl.when(pb != first + part)
            def _(part=part):
                col_copy(part, pb).start()

        @pl.loop(first, pb)
        def _(target):
            fold_copy(pb, target).start()

        def turn_chunk(n):
            return lax.rem(n + z // per_chunk, steps)

        def weight_turn(n, carry):
            t = turn_chunk(n)
            out = jnp.zeros((CHUNK, cols), jnp.float32)
            for h in range(heads):
                weights = []
                for m in range(pieces):
                    at = piece_rows(t, m)
                    student = st_ref[h, at, :]
                    grad = student - s_ref[h, at, :] * scaling[h : h + 1, :]
                    weights.append((grad * dec_ref[h, at, :]).astype(jnp.bfloat16))
                weight = jnp.concatenate(weights, axis=0)
                w_ref[h, chunk_rows(t), :] = weight
                out = out + dot(weight, ch_ref[h], ((1,), (0,)))
            gbpart_ref[pl.ds(t * per_chunk, per_chunk)] = (out * factor).reshape(
                per_chunk, 2, gb_rows, cols
            )
            gx_copy(t * per_chunk, per_chunk).start()

            @pl.when(n > 0)
            def _():
                send_grad_b(turn_chunk(n - 1))

            return carry

        lax.fori_loop(0, steps, weight_turn, 0)

        flats = []
        for h in range(heads):
            slope_ref[ka, h : h + 1, 0:qn] = jnp.sum(
                rs_ref[h, 0], axis=0, keepdims=True
            ) - scaling[h : h + 1, :] * jnp.sum(rs_ref[h, 1], axis=0, keepdims=True)
            flats.append(
                dot(bt_ref[h * state : (h + 1) * state, :], w_ref[h], ((1,), (0,)))
            )
        send_grad_b(turn_chunk(steps - 1))
        gcown_ref[...] = jnp.transpose(jnp.concatenate(flats, axis=0) * factor)
        gcsend_ref[...] = (
            gcown_ref[...].reshape(na, gc_rows, cols).astype(jnp.bfloat16)
        )

        @pl.loop(1, na)
        def _(k):
            gc_copy(ka, lax.rem(ka + k, na)).start()

        def later_turn(slot, total):
            fold_copy(slot, pb).wait_recv()
            return total + fold_ref[slot]

        slope_ref[ka, :, qn:] = lax.fori_loop(
            pb + 1, nb, later_turn, jnp.zeros((heads, 128), jnp.float32)
        )

        @pl.when(diagonal)
        def _():
            def col_turn(slot, total):
                col_copy(0, slot).wait_recv()
                return total + col_ref[slot]

            others = lax.fori_loop(
                first, pb, col_turn, jnp.zeros(col_ref.shape[1:], jnp.float32)
            )
            others = lax.fori_loop(pb + 1, nb, col_turn, others)
            everything = others + cs_ref[pl.ds(core * half, half)]
            for k in range(half):
                lanes = slice(k * 128, (k + 1) * 128)
                slope_ref[ka, :, lanes] = slope_ref[ka, :, lanes] - everything[k]

            @pl.when(core == 0)
            def _():
                slope_ref[ka, :, qn:] = jnp.sum(others, axis=0)

        @pl.loop(1, na)
        def _(k):
            slope_copy(ka, lax.rem(ka + k, na)).start()

    @pl.when(live)
    def _():
        gc_ref[...] = gcown_ref[
            pl.ds(pl.multiple_of(ka * gc_rows, gc_rows), gc_rows), :
        ]
        gb_ref[...] = gbown_ref[...]

    @pl.when(jnp.logical_not(live))
    def _():
        gc_ref[...] = jnp.zeros_like(gc_ref)
        gb_ref[...] = jnp.zeros_like(gb_ref)

    def gc_turn(slot, total):
        gc_copy(slot, slot).wait_recv()
        return total + gcrecv_ref[slot].astype(jnp.float32)

    sums = lax.fori_loop(0, jnp.minimum(ka, z + 1), gc_turn, gc_ref[...])
    gc_ref[...] = lax.fori_loop(ka + 1, z + 1, gc_turn, sums)

    def gb_turn(slot, total):
        gb_copy(slot, slot).wait_recv()
        return total + gbrecv_ref[slot].astype(jnp.float32)

    sums = lax.fori_loop(ka, z, gb_turn, gb_ref[...])
    gb_ref[...] = lax.fori_loop(jnp.maximum(ka, z + 1), nz, gb_turn, sums)

    @pl.when(live)
    def _():
        to(
            gbpart_ref.at[pl.ds(0, nz), other], gbsib_ref, gx_send, gx_recv.at[0], (sibling, ka)
        ).wait_send()

        for part in range(2):

            @pl.when(pb != first + part)
            def _(part=part):
                col_copy(part, pb).wait_send()

        @pl.loop(pb + 1, nb)
        def _(target):
            @pl.when(diagonal)
            def _():
                krate_copy(core, target).wait_send()

            @pl.when(jnp.logical_not(diagonal))
            def _():
                rfold_copy(pb, target).wait_send()

        @pl.loop(first, pb)
        def _(target):
            fold_copy(pb, target).wait_send()

        @pl.loop(0, z + 1)
        def _(target):
            @pl.when(target != ka)
            def _():
                stat_copy(ka, target).wait_send()

        rest = pl.ds(0, na - 1)
        to(gcsend_ref.at[rest], gcrecv_ref.at[rest], gc_send, gc_recv.at[0], (pb, ka)).wait_send()
        rest = pl.ds(0, nz - 1)
        to(gbsend_ref.at[rest], gbrecv_ref.at[rest], gb_send, gb_recv.at[0], (pb, ka)).wait_send()

    def slope_turn(slot, total):
        slope_copy(slot, slot).wait_recv()
        return total + slope_ref[slot]

    @pl.when(jnp.logical_not(live))
    def _():
        slope_ref[ka] = jnp.zeros(slope_ref.shape[1:], jnp.float32)

    both = lax.fori_loop(0, jnp.minimum(ka, z + 1), slope_turn, slope_ref[ka])
    both = lax.fori_loop(ka + 1, z + 1, slope_turn, both)
    slope = both[:, 0:qn]
    after = jnp.sum(both[:, qn:], axis=1, keepdims=True)
    scan_ref[...] = jnp.zeros_like(scan_ref)
    scan_ref[0:heads, :] = slope
    suffix = jnp.sum(slope, axis=1, keepdims=True) - lane_prefix(scan_ref[...])[0:heads, :]
    gr_ref[...] = -factor * (suffix + slope + after)

    @pl.when(live)
    def _():
        rest = pl.ds(0, na - 1)
        to(slope_ref.at[rest], slope_ref.at[rest], slope_send, slope_recv.at[0], (pb, ka)).wait_send()


def place(gc_in, gb_in, gr_in, gc_out, gb_out, gr_out, gc, gb, gr, sem):
    triples = ((gc_in, gc, gc_out), (gb_in, gb, gb_out), (gr_in, gr, gr_out))
    loads = [
        pltpu.make_async_copy(src, held, sem.at[n])
        for n, (src, held, _) in enumerate(triples)
    ]
    stores = [
        pltpu.make_async_copy(held, dst, sem.at[n])
        for n, (_, held, dst) in enumerate(triples)
    ]
    for load in loads:
        load.start()
    for load, store in zip(loads, stores):
        load.wait()
        store.start()
    for store in stores:
        store.wait()


def body(teacher_query, teacher_key, student_c, student_b, decay_rate):
    heads = decay_rate.shape[0]
    nb = lax.axis_size("pb")
    na = lax.axis_size("ka")
    qn, width = teacher_query.shape
    kn = teacher_key.shape[0]
    cols = student_c.shape[1]
    nz = nb // 2
    steps = kn // CHUNK
    f32, bf16 = jnp.float32, jnp.bfloat16
    vmem = pl.BlockSpec(memory_space=pltpu.VMEM)
    hbm = pl.BlockSpec(memory_space=pl.ANY)
    dma = pltpu.SemaphoreType.DMA
    scan_rows = -(-heads * 3 // 8) * 8
    shapes = (
        jax.ShapeDtypeStruct((qn // na, cols), f32),
        jax.ShapeDtypeStruct((kn // nb, cols), f32),
        jax.ShapeDtypeStruct((heads, qn), f32),
    )
    results = pl.pallas_call(
        functools.partial(kernel, nb, na, heads),
        out_shape=shapes,
        in_specs=[hbm, hbm, hbm, hbm, hbm],
        out_specs=[vmem, vmem, vmem],
        scratch_shapes=[
            pltpu.VMEM((qn, width), bf16),
            pltpu.VMEM((kn, width), bf16),
            pltpu.VMEM((qn, cols), bf16),
            pltpu.VMEM((kn, cols), bf16),
            pltpu.VMEM((heads, qn, cols), bf16),
            pltpu.VMEM((cols, kn), bf16),
            pltpu.VMEM((heads, kn, qn), f32),
            pltpu.VMEM((heads, kn, qn), f32),
            pltpu.VMEM((heads, kn, qn), f32),
            pltpu.VMEM((heads, kn, qn), bf16),
            pltpu.VMEM((heads, kn, 128), f32),
            pltpu.VMEM((scan_rows, qn), f32),
            pltpu.VMEM((heads, qn), f32),
            pltpu.VMEM((2, heads, qn), f32),
            pltpu.VMEM((nb, heads, 128), f32),
            pltpu.VMEM((na, heads, qn), f32),
            pltpu.VMEM((heads, qn), f32),
            pltpu.VMEM((kn // 128, heads, 128), f32),
            pltpu.VMEM((nb, heads, 128), f32),
            pltpu.VMEM((nb, qn // 128, heads, 128), f32),
            pltpu.VMEM((na, heads, qn + 128), f32),
            pltpu.VMEM((heads, 2, 8, qn), f32),
            pltpu.VMEM((nz, 2, kn // nb, cols), f32),
            pltpu.VMEM((nz, kn // nb, cols), f32),
            pltpu.VMEM((kn // nb, cols), f32),
            pltpu.VMEM((nz, kn // nb, cols), bf16),
            pltpu.VMEM((nz, kn // nb, cols), bf16),
            pltpu.VMEM((qn, cols), f32),
            pltpu.VMEM((na, qn // na, cols), bf16),
            pltpu.VMEM((na, qn // na, cols), bf16),
            dma((5,)),
            dma((nb,)),
            dma((2,)),
            dma((nb,)),
            dma((na,)),
            dma((na,)),
            dma((nb,)),
            dma((nb,)),
            dma((2,)),
            dma((nb,)),
            dma,
            dma((na,)),
            dma,
            dma((steps,)),
            dma,
            dma((nz,)),
            dma,
            dma((na,)),
        ],
        compiler_params=pltpu.CompilerParams(
            collective_id=0, has_side_effects=True, vmem_limit_bytes=62 * 1024 * 1024
        ),
    )(teacher_query, teacher_key, student_c, student_b, decay_rate)
    return pl.pallas_call(
        place,
        out_shape=shapes,
        in_specs=[hbm, hbm, hbm],
        out_specs=[hbm, hbm, hbm],
        scratch_shapes=[pltpu.VMEM(shape.shape, f32) for shape in shapes] + [dma((3,))],
        compiler_params=pltpu.CompilerParams(vmem_limit_bytes=62 * 1024 * 1024),
    )(*results)


def solution(mesh):
    placed = (P("pb", None), P("ka", None), P("pb", None), P("ka", None), P(None, "pb"))
    return jax.shard_map(
        body,
        mesh=mesh,
        in_specs=placed,
        out_specs=(P(("pb", "ka"), None), P(("ka", "pb"), None), P(None, "pb")),
        check_vma=False,
    )
```

```python
import functools
import math

import jax
import jax.numpy as jnp
from jax import lax
from jax.experimental import pallas as pl
from jax.experimental.pallas import tpu as pltpu
from jax.sharding import PartitionSpec as P

MESH = pl.DeviceIdType.MESH
NEGATIVE = -1e30
LOG2E = 1.0 / math.log(2.0)
CHUNK = 256
PIECE = 16


def dot(a, b, dims):
    return lax.dot_general(a, b, (dims, ((), ())), preferred_element_type=jnp.float32)


def fold_rows(x):
    return jnp.sum(x.reshape(x.shape[0] // 8, 8, x.shape[1]), axis=0)


def fold_lanes(x):
    width = x.shape[1]
    out = x[:, 0:128]
    for k in range(128, width, 128):
        out = out + x[:, k : k + 128]
    return out


def lane_prefix(x):
    width = x.shape[1]
    lane = lax.broadcasted_iota(jnp.int32, x.shape, 1)
    shift = 1
    while shift < width:
        x = x + jnp.where(lane >= shift, pltpu.roll(x, shift, 1), 0.0)
        shift *= 2
    return x


def kernel(
    nb,
    na,
    heads,
    q_hbm,
    k_hbm,
    c_hbm,
    b_hbm,
    rate_hbm,
    gc_ref,
    gb_ref,
    gr_ref,
    q_ref,
    k_ref,
    c_ref,
    b_ref,
    ch_ref,
    bt_ref,
    s_ref,
    st_ref,
    dec_ref,
    w_ref,
    kcol_ref,
    scan_ref,
    rate_ref,
    krate_ref,
    rfold_ref,
    stat_ref,
    peak_ref,
    total_ref,
    mix_ref,
    scale_ref,
    cs_ref,
    fold_ref,
    col_ref,
    slope_ref,
    rs_ref,
    gbpart_ref,
    gbsib_ref,
    gbown_ref,
    gbsend_ref,
    gbrecv_ref,
    gcown_ref,
    gcsend_ref,
    gcrecv_ref,
    in_sem,
    rate_send,
    krate_recv,
    rfold_recv,
    stat_send,
    stat_recv,
    fold_send,
    fold_recv,
    col_send,
    col_recv,
    slope_send,
    slope_recv,
    gx_send,
    gx_recv,
    gb_send,
    gb_recv,
    gc_send,
    gc_recv,
):
    pb = lax.axis_index("pb")
    ka = lax.axis_index("ka")
    qn, width = q_ref.shape
    kn = k_ref.shape[0]
    dh = width // heads
    cols = c_ref.shape[1]
    state = cols // heads
    nz = nb // 2
    z = pb // 2
    core = lax.rem(pb, 2)
    other = 1 - core
    sibling = 2 * z + other
    steps = kn // CHUNK
    half = qn // 128
    pieces = CHUNK // PIECE
    blocks = CHUNK // 128
    gb_rows = kn // nb
    gc_rows = qn // na
    per_chunk = CHUNK // (2 * gb_rows)
    factor = 2.0 * qn * nb
    first = 2 * ka
    live = z >= ka
    diagonal = z == ka

    loads = [
        pltpu.make_async_copy(src, dst, in_sem.at[n])
        for n, (src, dst) in enumerate(
            (
                (q_hbm, q_ref),
                (k_hbm, k_ref),
                (rate_hbm, rate_ref),
                (c_hbm, c_ref),
                (b_hbm, b_ref),
            )
        )
    ]
    for load in loads:
        load.start()

    barrier = pltpu.get_barrier_semaphore()

    @pl.loop(1, na)
    def _(k):
        pl.semaphore_signal(
            barrier, inc=1, device_id=(pb, lax.rem(ka + k, na)), device_id_type=MESH
        )

    @pl.loop(1, nb)
    def _(k):
        pl.semaphore_signal(
            barrier, inc=1, device_id=(lax.rem(pb + k, nb), ka), device_id_type=MESH
        )

    def to(src, dst, send, recv, device):
        return pltpu.make_async_remote_copy(
            src_ref=src,
            dst_ref=dst,
            send_sem=send,
            recv_sem=recv,
            device_id=device,
            device_id_type=MESH,
        )

    def up(target):
        return (2 * target + core, ka)

    def krate_copy(slot, target):
        return to(
            rate_ref,
            krate_ref.at[slot],
            rate_send.at[target],
            krate_recv.at[slot],
            (target, ka),
        )

    def rfold_copy(slot, target):
        return to(
            rfold_ref.at[slot],
            rfold_ref.at[slot],
            rate_send.at[target],
            rfold_recv.at[slot],
            (target, ka),
        )

    def stat_copy(slot, target):
        return to(
            stat_ref.at[slot],
            stat_ref.at[slot],
            stat_send.at[target],
            stat_recv.at[slot],
            (pb, target),
        )

    def fold_copy(slot, target):
        return to(
            fold_ref.at[slot],
            fold_ref.at[slot],
            fold_send.at[target],
            fold_recv.at[slot],
            (target, ka),
        )

    def col_copy(part, slot):
        return to(
            cs_ref.at[pl.ds(part * half, half)],
            col_ref.at[slot],
            col_send.at[part],
            col_recv.at[slot],
            (first + part, ka),
        )

    def slope_copy(slot, target):
        return to(
            slope_ref.at[slot],
            slope_ref.at[slot],
            slope_send,
            slope_recv.at[slot],
            (pb, target),
        )

    def gx_copy(start, count):
        return to(
            gbpart_ref.at[pl.ds(start, count), other],
            gbsib_ref.at[pl.ds(start, count)],
            gx_send,
            gx_recv.at[start // per_chunk],
            (sibling, ka),
        )

    def gb_copy(slot, target):
        return to(
            gbsend_ref.at[target],
            gbrecv_ref.at[slot],
            gb_send,
            gb_recv.at[slot],
            up(target),
        )

    def gc_copy(slot, target):
        return to(
            gcsend_ref.at[target],
            gcrecv_ref.at[slot],
            gc_send,
            gc_recv.at[slot],
            (pb, target),
        )

    offset = pb * qn - ka * kn

    def mask_of(t, piece):
        rows = lax.broadcasted_iota(jnp.int32, (PIECE, qn), 0)
        lanes = lax.broadcasted_iota(jnp.int32, (PIECE, qn), 1)
        return lanes - rows >= t * CHUNK + piece * PIECE - offset

    def piece_rows(t, piece):
        return pl.ds(pl.multiple_of(t * CHUNK + piece * PIECE, PIECE), PIECE)

    def chunk_rows(t):
        return pl.ds(pl.multiple_of(t * CHUNK, CHUNK), CHUNK)

    scale2 = LOG2E / math.sqrt(dh)

    def stats(masked):
        def score_turn(t, carry):
            rows = chunk_rows(t)
            every = [
                dot(
                    k_ref[rows, h * dh : (h + 1) * dh],
                    q_ref[:, h * dh : (h + 1) * dh],
                    ((1,), (1,)),
                )
                for h in range(heads)
            ]
            for h in range(heads):
                parts = []
                peak = jnp.full((8, qn), NEGATIVE, jnp.float32)
                for n in range(pieces):
                    part = every[h][n * PIECE : (n + 1) * PIECE]
                    if masked:
                        part = jnp.where(mask_of(t, n), part, NEGATIVE)
                    parts.append(part)
                    for k in range(0, PIECE, 8):
                        peak = jnp.maximum(peak, part[k : k + 8])
                peak = jnp.max(peak, axis=0, keepdims=True)
                total = jnp.zeros((8, qn), jnp.float32)
                for n in range(pieces):
                    e = jnp.exp2((parts[n] - peak) * scale2)
                    s_ref[h, piece_rows(t, n), :] = e
                    for k in range(0, PIECE, 8):
                        total = total + e[k : k + 8]
                peak_ref[t, h : h + 1, :] = peak * scale2
                total_ref[t, h : h + 1, :] = jnp.sum(total, axis=0, keepdims=True)
            return carry

        lax.fori_loop(0, steps, score_turn, 0)
        peaks = peak_ref[...]
        peak = jnp.max(peaks, axis=0)
        total = jnp.sum(total_ref[...] * jnp.exp2(peaks - peak[None]), axis=0)
        stat_ref[ka] = peak + jnp.log2(total)

    @pl.when(live)
    def _():
        stat_init = jnp.full((heads, qn), NEGATIVE, jnp.float32)

        @pl.loop(z + 1, na)
        def _(slot):
            stat_ref[slot] = stat_init

    loads[0].wait()
    loads[1].wait()

    @pl.when(diagonal)
    def _():
        stats(True)

    @pl.when(z > ka)
    def _():
        stats(False)

    for load in loads[2:]:
        load.wait()
    pl.semaphore_wait(barrier, na + nb - 2)

    @pl.when(live)
    def _():
        rfold_ref[pb] = fold_lanes(rate_ref[...])

        @pl.loop(pb + 1, nb)
        def _(target):
            @pl.when(diagonal)
            def _():
                krate_copy(core, target).start()

            @pl.when(jnp.logical_not(diagonal))
            def _():
                rfold_copy(pb, target).start()

        @pl.loop(1, na)
        def _(k):
            target = lax.rem(ka + k, na)

            @pl.when(target <= z)
            def _():
                stat_copy(ka, target).start()

        head_of = lax.broadcasted_iota(jnp.int32, (qn, cols), 1) // state
        c_all = c_ref[...]
        for h in range(heads):
            ch_ref[h] = jnp.where(head_of == h, c_all, jnp.zeros_like(c_all))
        bt_ref[...] = jnp.transpose(b_ref[...])

        @pl.when(diagonal)
        def _():
            krate_ref[core] = rate_ref[...]

            @pl.when(core == 0)
            def _():
                krate_ref[1] = jnp.zeros_like(rate_ref)

        @pl.when(pb > first)
        def _():
            krate_copy(0, pb).wait_recv()

        @pl.when(z > ka)
        def _():
            krate_copy(1, pb).wait_recv()

        scan_ref[...] = jnp.zeros_like(scan_ref)
        scan_ref[0:heads, :] = rate_ref[...]
        for part in range(2):
            low = heads * (1 + part)
            scan_ref[low : low + heads, :] = krate_ref[part]

        rates = scan_ref[...]
        scan_ref[...] = lane_prefix(rates)
        ends = jnp.sum(rates, axis=1, keepdims=True)
        for h in range(heads):
            shift = jnp.zeros((1, 1), jnp.float32)
            for part in range(2):
                row = heads * (1 + part) + h
                prefix = (scan_ref[row : row + 1, :] + shift) * LOG2E
                kcol_ref[h, part * qn : (part + 1) * qn, :] = jnp.transpose(
                    jnp.broadcast_to(prefix, (128, qn))
                )
                shift = shift + ends[row : row + 1, :]

        def between_turn(slot, total):
            rfold_copy(slot, pb).wait_recv()
            return total + rfold_ref[slot]

        between = lax.fori_loop(
            first + 2, pb, between_turn, jnp.zeros((heads, 128), jnp.float32)
        )
        before = (
            jnp.sum(between, axis=1, keepdims=True)
            + jnp.where(pb > first, ends[heads : 2 * heads], 0.0)
            + jnp.where(z > ka, ends[2 * heads : 3 * heads], 0.0)
        )
        arow = (scan_ref[0:heads, :] + before) * LOG2E

        def student_pass(masked):
            def student_turn(t, sums):
                b_rows = b_ref[chunk_rows(t), :]
                inners = [dot(b_rows, ch_ref[h], ((1,), (1,))) for h in range(heads)]
                new_sums = []
                for h in range(heads):
                    squares = sums[h]
                    mixed = jnp.zeros((8, qn), jnp.float32)
                    for m in range(pieces):
                        at = piece_rows(t, m)
                        column = kcol_ref[h, at, :]
                        gap = (
                            jnp.concatenate([column] * (qn // 128), axis=1)
                            - arow[h : h + 1, :]
                        )
                        if masked:
                            gap = jnp.where(mask_of(t, m), gap, NEGATIVE)
                        decay = jnp.exp2(gap)
                        student = inners[h][m * PIECE : (m + 1) * PIECE] * decay
                        dec_ref[h, at, :] = decay
                        st_ref[h, at, :] = student
                        square = student * student
                        mix = student * s_ref[h, at, :]
                        for k in range(0, PIECE, 8):
                            squares = squares + square[k : k + 8]
                            mixed = mixed + mix[k : k + 8]
                    new_sums.append(squares)
                    mix_ref[t, h : h + 1, :] = jnp.sum(mixed, axis=0, keepdims=True)
                return tuple(new_sums)

            zero = jnp.zeros((8, qn), jnp.float32)
            sums = lax.fori_loop(
                0, steps, student_turn, tuple(zero for _ in range(heads))
            )
            for h in range(heads):
                rs_ref[h] = sums[h]

        @pl.when(diagonal)
        def _():
            student_pass(True)

        @pl.when(z > ka)
        def _():
            student_pass(False)

        @pl.loop(0, z + 1)
        def _(slot):
            @pl.when(slot != ka)
            def _():
                stat_copy(slot, slot).wait_recv()

        parts = stat_ref[...]
        peak = jnp.max(parts, axis=0)
        total = jnp.sum(jnp.exp2(parts - peak[None]), axis=0)
        scale_ref[...] = jnp.exp2(peak_ref[...] - (peak + jnp.log2(total))[None])

        def send_grad_b(t):
            gx_copy(t * per_chunk, per_chunk).wait_recv()

            @pl.loop(0, per_chunk)
            def _(k):
                target = t * per_chunk + k
                sums = gbpart_ref[target, core] + gbsib_ref[target]

                @pl.when(target == z)
                def _():
                    gbown_ref[...] = sums

                @pl.when(target != z)
                def _():
                    gbsend_ref[target] = sums.astype(jnp.bfloat16)
                    gb_copy(z, target).start()

        def column_turn(t, carry):
            for h in range(heads):
                folds = []
                scaling = scale_ref[t, h : h + 1, :]
                for m in range(pieces):
                    at = piece_rows(t, m)
                    student = st_ref[h, at, :]
                    grad = student - s_ref[h, at, :] * scaling
                    folds.append(fold_lanes(grad * student))
                fold = jnp.concatenate(folds, axis=0)
                for k in range(blocks):
                    flipped = jnp.transpose(fold[k * 128 : (k + 1) * 128])
                    cs_ref[t * blocks + k, h : h + 1, :] = jnp.sum(
                        flipped, axis=0, keepdims=True
                    )
            return carry

        lax.fori_loop(0, steps, column_turn, 0)
        fold_ref[pb] = jnp.sum(cs_ref[...], axis=0)

        for part in range(2):

            @pl.when(pb != first + part)
            def _(part=part):
                col_copy(part, pb).start()

        @pl.loop(first, pb)
        def _(target):
            fold_copy(pb, target).start()

        def weight_turn(t, carry):
            out = jnp.zeros((CHUNK, cols), jnp.float32)
            for h in range(heads):
                weights = []
                scaling = scale_ref[t, h : h + 1, :]
                for m in range(pieces):
                    at = piece_rows(t, m)
                    student = st_ref[h, at, :]
                    grad = student - s_ref[h, at, :] * scaling
                    weights.append((grad * dec_ref[h, at, :]).astype(jnp.bfloat16))
                weight = jnp.concatenate(weights, axis=0)
                w_ref[h, chunk_rows(t), :] = weight
                out = out + dot(weight, ch_ref[h], ((1,), (0,)))
            gbpart_ref[pl.ds(t * per_chunk, per_chunk)] = (out * factor).reshape(
                per_chunk, 2, gb_rows, cols
            )
            gx_copy(t * per_chunk, per_chunk).start()

            @pl.when(t > 0)
            def _():
                send_grad_b(t - 1)

            return carry

        lax.fori_loop(0, steps, weight_turn, 0)

        flats = []
        for h in range(heads):
            slope_ref[ka, h : h + 1, 0:qn] = jnp.sum(rs_ref[h], axis=0, keepdims=True)
            flats.append(
                dot(bt_ref[h * state : (h + 1) * state, :], w_ref[h], ((1,), (0,)))
            )
        slope_ref[ka, :, 0:qn] = slope_ref[ka, :, 0:qn] - jnp.sum(
            scale_ref[...] * mix_ref[...], axis=0
        )
        send_grad_b(steps - 1)
        gcown_ref[...] = jnp.transpose(jnp.concatenate(flats, axis=0) * factor)
        gcsend_ref[...] = (
            gcown_ref[...].reshape(na, gc_rows, cols).astype(jnp.bfloat16)
        )

        @pl.loop(1, na)
        def _(k):
            gc_copy(ka, lax.rem(ka + k, na)).start()

        def later_turn(slot, total):
            fold_copy(slot, pb).wait_recv()
            return total + fold_ref[slot]

        slope_ref[ka, :, qn:] = lax.fori_loop(
            pb + 1, nb, later_turn, jnp.zeros((heads, 128), jnp.float32)
        )

        @pl.when(diagonal)
        def _():
            def col_turn(slot, total):
                col_copy(0, slot).wait_recv()
                return total + col_ref[slot]

            others = lax.fori_loop(
                first, pb, col_turn, jnp.zeros(col_ref.shape[1:], jnp.float32)
            )
            others = lax.fori_loop(pb + 1, nb, col_turn, others)
            everything = others + cs_ref[pl.ds(core * half, half)]
            for k in range(half):
                lanes = slice(k * 128, (k + 1) * 128)
                slope_ref[ka, :, lanes] = slope_ref[ka, :, lanes] - everything[k]

            @pl.when(core == 0)
            def _():
                slope_ref[ka, :, qn:] = jnp.sum(others, axis=0)

        @pl.loop(1, na)
        def _(k):
            slope_copy(ka, lax.rem(ka + k, na)).start()

    @pl.when(live)
    def _():
        gc_ref[...] = gcown_ref[
            pl.ds(pl.multiple_of(ka * gc_rows, gc_rows), gc_rows), :
        ]
        gb_ref[...] = gbown_ref[...]

    @pl.when(jnp.logical_not(live))
    def _():
        gc_ref[...] = jnp.zeros_like(gc_ref)
        gb_ref[...] = jnp.zeros_like(gb_ref)

    def gc_turn(slot, total):
        gc_copy(slot, slot).wait_recv()
        return total + gcrecv_ref[slot].astype(jnp.float32)

    sums = lax.fori_loop(0, jnp.minimum(ka, z + 1), gc_turn, gc_ref[...])
    gc_ref[...] = lax.fori_loop(ka + 1, z + 1, gc_turn, sums)

    def slope_turn(slot, total):
        slope_copy(slot, slot).wait_recv()
        return total + slope_ref[slot]

    @pl.when(jnp.logical_not(live))
    def _():
        slope_ref[ka] = jnp.zeros(slope_ref.shape[1:], jnp.float32)

    both = lax.fori_loop(0, jnp.minimum(ka, z + 1), slope_turn, slope_ref[ka])
    both = lax.fori_loop(ka + 1, z + 1, slope_turn, both)
    slope = both[:, 0:qn]
    after = jnp.sum(both[:, qn:], axis=1, keepdims=True)
    scan_ref[...] = jnp.zeros_like(scan_ref)
    scan_ref[0:heads, :] = slope
    suffix = jnp.sum(slope, axis=1, keepdims=True) - lane_prefix(scan_ref[...])[0:heads, :]
    gr_ref[...] = -factor * (suffix + slope + after)

    @pl.when(live)
    def _():
        to(
            gbpart_ref.at[pl.ds(0, nz), other], gbsib_ref, gx_send, gx_recv.at[0], (sibling, ka)
        ).wait_send()

        for part in range(2):

            @pl.when(pb != first + part)
            def _(part=part):
                col_copy(part, pb).wait_send()

        @pl.loop(pb + 1, nb)
        def _(target):
            @pl.when(diagonal)
            def _():
                krate_copy(core, target).wait_send()

            @pl.when(jnp.logical_not(diagonal))
            def _():
                rfold_copy(pb, target).wait_send()

        @pl.loop(first, pb)
        def _(target):
            fold_copy(pb, target).wait_send()

        @pl.loop(0, z + 1)
        def _(target):
            @pl.when(target != ka)
            def _():
                stat_copy(ka, target).wait_send()

        rest = pl.ds(0, na - 1)
        to(gcsend_ref.at[rest], gcrecv_ref.at[rest], gc_send, gc_recv.at[0], (pb, ka)).wait_send()
        rest = pl.ds(0, nz - 1)
        to(gbsend_ref.at[rest], gbrecv_ref.at[rest], gb_send, gb_recv.at[0], (pb, ka)).wait_send()

    def gb_turn(slot, total):
        gb_copy(slot, slot).wait_recv()
        return total + gbrecv_ref[slot].astype(jnp.float32)

    sums = lax.fori_loop(ka, z, gb_turn, gb_ref[...])
    gb_ref[...] = lax.fori_loop(jnp.maximum(ka, z + 1), nz, gb_turn, sums)

    @pl.when(live)
    def _():
        rest = pl.ds(0, na - 1)
        to(slope_ref.at[rest], slope_ref.at[rest], slope_send, slope_recv.at[0], (pb, ka)).wait_send()


def place(gc_in, gb_in, gr_in, gc_out, gb_out, gr_out, gc, gb, gr, sem):
    triples = ((gc_in, gc, gc_out), (gb_in, gb, gb_out), (gr_in, gr, gr_out))
    loads = [
        pltpu.make_async_copy(src, held, sem.at[n])
        for n, (src, held, _) in enumerate(triples)
    ]
    stores = [
        pltpu.make_async_copy(held, dst, sem.at[n])
        for n, (_, held, dst) in enumerate(triples)
    ]
    for load in loads:
        load.start()
    for load, store in zip(loads, stores):
        load.wait()
        store.start()
    for store in stores:
        store.wait()


def body(teacher_query, teacher_key, student_c, student_b, decay_rate):
    heads = decay_rate.shape[0]
    nb = lax.axis_size("pb")
    na = lax.axis_size("ka")
    qn, width = teacher_query.shape
    kn = teacher_key.shape[0]
    cols = student_c.shape[1]
    nz = nb // 2
    steps = kn // CHUNK
    f32, bf16 = jnp.float32, jnp.bfloat16
    vmem = pl.BlockSpec(memory_space=pltpu.VMEM)
    hbm = pl.BlockSpec(memory_space=pl.ANY)
    dma = pltpu.SemaphoreType.DMA
    scan_rows = -(-heads * 3 // 8) * 8
    shapes = (
        jax.ShapeDtypeStruct((qn // na, cols), f32),
        jax.ShapeDtypeStruct((kn // nb, cols), f32),
        jax.ShapeDtypeStruct((heads, qn), f32),
    )
    results = pl.pallas_call(
        functools.partial(kernel, nb, na, heads),
        out_shape=shapes,
        in_specs=[hbm, hbm, hbm, hbm, hbm],
        out_specs=[vmem, vmem, vmem],
        scratch_shapes=[
            pltpu.VMEM((qn, width), bf16),
            pltpu.VMEM((kn, width), bf16),
            pltpu.VMEM((qn, cols), bf16),
            pltpu.VMEM((kn, cols), bf16),
            pltpu.VMEM((heads, qn, cols), bf16),
            pltpu.VMEM((cols, kn), bf16),
            pltpu.VMEM((heads, kn, qn), f32),
            pltpu.VMEM((heads, kn, qn), f32),
            pltpu.VMEM((heads, kn, qn), f32),
            pltpu.VMEM((heads, kn, qn), bf16),
            pltpu.VMEM((heads, kn, 128), f32),
            pltpu.VMEM((scan_rows, qn), f32),
            pltpu.VMEM((heads, qn), f32),
            pltpu.VMEM((2, heads, qn), f32),
            pltpu.VMEM((nb, heads, 128), f32),
            pltpu.VMEM((na, heads, qn), f32),
            pltpu.VMEM((steps, heads, qn), f32),
            pltpu.VMEM((steps, heads, qn), f32),
            pltpu.VMEM((steps, heads, qn), f32),
            pltpu.VMEM((steps, heads, qn), f32),
            pltpu.VMEM((kn // 128, heads, 128), f32),
            pltpu.VMEM((nb, heads, 128), f32),
            pltpu.VMEM((nb, qn // 128, heads, 128), f32),
            pltpu.VMEM((na, heads, qn + 128), f32),
            pltpu.VMEM((heads, 8, qn), f32),
            pltpu.VMEM((nz, 2, kn // nb, cols), f32),
            pltpu.VMEM((nz, kn // nb, cols), f32),
            pltpu.VMEM((kn // nb, cols), f32),
            pltpu.VMEM((nz, kn // nb, cols), bf16),
            pltpu.VMEM((nz, kn // nb, cols), bf16),
            pltpu.VMEM((qn, cols), f32),
            pltpu.VMEM((na, qn // na, cols), bf16),
            pltpu.VMEM((na, qn // na, cols), bf16),
            dma((5,)),
            dma((nb,)),
            dma((2,)),
            dma((nb,)),
            dma((na,)),
            dma((na,)),
            dma((nb,)),
            dma((nb,)),
            dma((2,)),
            dma((nb,)),
            dma,
            dma((na,)),
            dma,
            dma((steps,)),
            dma,
            dma((nz,)),
            dma,
            dma((na,)),
        ],
        compiler_params=pltpu.CompilerParams(
            collective_id=0, has_side_effects=True, vmem_limit_bytes=62 * 1024 * 1024
        ),
    )(teacher_query, teacher_key, student_c, student_b, decay_rate)
    return pl.pallas_call(
        place,
        out_shape=shapes,
        in_specs=[hbm, hbm, hbm],
        out_specs=[hbm, hbm, hbm],
        scratch_shapes=[pltpu.VMEM(shape.shape, f32) for shape in shapes] + [dma((3,))],
        compiler_params=pltpu.CompilerParams(vmem_limit_bytes=62 * 1024 * 1024),
    )(*results)


def solution(mesh):
    placed = (P("pb", None), P("ka", None), P("pb", None), P("ka", None), P(None, "pb"))
    return jax.shard_map(
        body,
        mesh=mesh,
        in_specs=placed,
        out_specs=(P(("pb", "ka"), None), P(("ka", "pb"), None), P(None, "pb")),
        check_vma=False,
    )
```
